128 devices in a mesh: north: 8 (over z, core), east: 16 (over y, x).
Axes of the slice: x: 4, y: 4, z: 4, core: 2. Of those that a mesh axis runs over, the one named last changes fastest.
Arguments:
- gates: bfloat16 [32768, 16, 128], P(('north', 'east')), may hold values from -6 to 6
- mixing_weight_blocks: bfloat16 [32768, 128, 128], P(('north', 'east')), may hold values from -0.5 to 0.5
- send_pick: int32 [128, 128, 2], P(('north', 'east')), may hold values from -1 to 255, as said below
- feed: int32 [128, 256], P(('north', 'east')), may hold values from -1 to 255, as said below
- window: int32 [128, 256], P(('north', 'east')), may hold values from 0 to 127, as said below
- proj_weight: bfloat16 [64, 64], replicated, may hold values from -0.75 to 0.75
- conv_weight: bfloat16 [3, 9, 64, 64], replicated, may hold values from -0.25 to 0.25
- rates: int32 [3], replicated, may hold values from 1 to 4, as said below
Outputs:
- nowcast_features: bfloat16 [64, 256, 2048], P(None, 'north', 'east')
The draws below stay inside these ranges and needn't reach their ends.
Inputs may be any that keep to these rules, and one draw needn't show every extreme that they name: `send_pick`: -1 marks an empty slot; other entries are the source device's own sweep blocks, distinct within one source and destination, filled slots first; some source fills all 2 slots to some owner. `feed`: -1 marks padding; every filled slot sent to an owner is named exactly once in its list and no empty slot is named; used entries come first, at least 128 of them in every list; some owner has all 256 entries used. Every window of every owner's tile is named by at least one used entry of that owner's list. `rates`: some layer has rate 4.
All inputs are finite; a program needn't handle non-finite values.
Results may differ from the reference program's by a relative error of at most 0.0063.
Values may be sent and summed in bfloat16 or wider, within the bound.
A program may use at most 128 MiB of HBM per device.

```python
import jax
import jax.numpy as jnp
from jax import lax

GATES = 128
FEATS = 16
CHANNELS = 64
ROWS = 64
COLS = 256
WIN_R = 8
WIN_C = 16
NWIN = 128
SB = 256
PMAX = 256
NDEV = 128
CAP = 2
DMAX = 4
LAYERS = 3
N_NORTH = 8
N_EAST = 16


def routing_tables(key):
    base = jax.random.fold_in(key, 7)
    key_a, key_b, key_c, key_d, key_e, key_f = jax.random.split(base, 6)
    span = PMAX - NWIN
    extras = jax.random.randint(key_a, (4, NDEV), 0, span + 1)
    totals = NWIN + jnp.min(extras, axis=0)
    heavy = jax.random.randint(key_b, (), 0, NDEV)
    totals = totals.at[heavy].set(PMAX)
    orders = jax.vmap(lambda k: jax.random.permutation(k, NDEV))(jax.random.split(key_c, NDEV))
    ranks = jnp.argsort(orders, axis=1)
    counts = jnp.clip(totals[:, None] - ranks * CAP, 0, CAP)
    counts = counts.T
    pick_keys = jax.random.split(key_d, NDEV * NDEV)
    picks = jax.vmap(lambda k: jax.random.permutation(k, SB)[:CAP])(pick_keys).reshape(NDEV, NDEV, CAP)
    slot_pos = jnp.arange(CAP)[None, None, :]
    send_pick = jnp.where(slot_pos < counts[:, :, None], picks, -1).astype(jnp.int32)
    slots_all = jnp.arange(NDEV * CAP)
    tie_keys = jax.random.split(key_e, NDEV)

    def owner_list(owner, tiebreak_key):
        used = slots_all % CAP < counts[slots_all // CAP, owner]
        ties = jax.random.permutation(tiebreak_key, NDEV * CAP)
        score = jnp.where(used, 0, NDEV * CAP) + ties
        order = jnp.argsort(score)[:PMAX]
        return jnp.where(jnp.arange(PMAX) < totals[owner], order, -1)
    feed = jax.vmap(owner_list)(jnp.arange(NDEV), tie_keys).astype(jnp.int32)
    win_keys = jax.random.split(key_f, NDEV)

    def owner_windows(win_key, total):
        key_p, key_q = jax.random.split(win_key)
        positions = jnp.arange(PMAX, dtype=jnp.int32)
        ties = jax.random.permutation(key_p, PMAX).astype(jnp.int32)
        score = jnp.where(positions < total, ties, PMAX + positions)
        placed = jnp.argsort(score)
        extra = jax.random.randint(key_q, (PMAX - NWIN,), 0, NWIN).astype(jnp.int32)
        values = jnp.concatenate([jnp.arange(NWIN, dtype=jnp.int32), extra])
        return jnp.zeros((PMAX,), jnp.int32).at[placed].set(values)
    window = jax.vmap(owner_windows)(win_keys, totals).astype(jnp.int32)
    return (send_pick, feed, window)


def draw_send_pick(key, part):
    return routing_tables(key)[0]


def draw_feed(key, part):
    return routing_tables(key)[1]


def draw_window(key, part):
    return routing_tables(key)[2]


def draw_rates(key, part):
    values = jax.random.randint(jax.random.fold_in(key, 11), (LAYERS,), 1, DMAX + 1)
    where_max = jax.random.randint(jax.random.fold_in(key, 12), (), 0, LAYERS)
    return values.at[where_max].set(DMAX).astype(jnp.int32)


def shard_levels(own_key, extent, shards, smallest, largest):
    level, own = 1.0, jax.random.fold_in(own_key, 6)
    for axis_at, shards_of in shards:
        draws = jnp.exp(jax.random.uniform(jax.random.fold_in(own, axis_at), (shards_of,), jnp.float32, smallest / len(shards), largest / len(shards)))
        level = level * jnp.repeat(draws, extent[axis_at] // shards_of).reshape([-1 if axis == axis_at else 1 for axis in range(len(extent))])
    return level


def scatter_about(own_key, shape, spread, most, cuts=(), kind=jnp.bfloat16):
    gain = shard_levels(own_key, shape, cuts, -0.22, 0.18) if cuts else 1.0
    result = jax.random.normal(own_key, shape, jnp.float32) * spread * gain
    return jnp.minimum(jnp.maximum(result, -most), most).astype(kind)


def setup_inputs(seed: int = 0) -> dict:
    splits = jax.random.split(jax.random.key(seed), 9)
    gates = scatter_about(splits[0], (NDEV * SB, FEATS, GATES), 1.0, 6.0, ((0, 128),))
    mixing_weight_blocks = scatter_about(splits[1], (NDEV * PMAX, GATES, WIN_R * WIN_C), GATES ** -0.5, 0.5, ((0, 128),))
    send_pick = draw_send_pick(jax.random.fold_in(splits[8], 71), 0)
    feed = draw_feed(jax.random.fold_in(splits[8], 71), 0)
    window = draw_window(jax.random.fold_in(splits[8], 71), 0)
    proj_weight = scatter_about(splits[5], (CHANNELS, 4 * FEATS), (4 * FEATS) ** -0.5, 0.75)
    conv_weight = scatter_about(splits[6], (LAYERS, 9, CHANNELS, CHANNELS), (9 * CHANNELS) ** -0.5, 0.25)
    rates = draw_rates(jax.random.fold_in(splits[8], 71), 0)
    return {"gates": gates, "mixing_weight_blocks": mixing_weight_blocks, "send_pick": send_pick, "feed": feed, "window": window, "proj_weight": proj_weight, "conv_weight": conv_weight, "rates": rates}


def dilated_filter_layer(feats, taps, rate):
    padded = jnp.pad(feats, ((0, 0), (DMAX, DMAX), (DMAX, DMAX)))
    band = ROWS // 2
    width = feats.shape[2]

    def one_band(index):
        piece = lax.dynamic_slice(padded, (jnp.int32(0), (index * band).astype(jnp.int32), jnp.int32(0)), (CHANNELS, band + 2 * DMAX, width + 2 * DMAX))
        total = jnp.zeros((CHANNELS, band * width), jnp.float32)
        for upper in range(3):
            for lower in range(3):
                start_r = (DMAX + (upper - 1) * rate).astype(jnp.int32)
                start_c = (DMAX + (lower - 1) * rate).astype(jnp.int32)
                sliced = lax.dynamic_slice(piece, (jnp.int32(0), start_r, start_c), (CHANNELS, band, width))
                total = total + jnp.dot(taps[upper * 3 + lower], sliced.reshape(CHANNELS, band * width), preferred_element_type=jnp.float32)
        return total.reshape(CHANNELS, band, width)

    bands = lax.map(one_band, jnp.arange(N_NORTH, dtype=jnp.int32))
    return bands.transpose(1, 0, 2, 3).reshape(CHANNELS, N_NORTH * band, width)


def reference(gates, mixing_weight_blocks, send_pick, feed, window, proj_weight, conv_weight, rates):
    ndev = N_NORTH * N_EAST
    nwin = (ROWS // WIN_R) * (COLS // WIN_C)

    def one_tile(owner):
        entries = feed[owner]
        used = entries >= 0
        slot_id = jnp.clip(entries, 0, ndev * CAP - 1)
        source = slot_id // CAP
        slot = slot_id % CAP
        block = send_pick[source, owner, slot]
        valid = used & (block >= 0)
        rowid = source * SB + jnp.clip(block, 0, SB - 1)
        selected_items = jnp.take(gates, rowid, axis=0).astype(jnp.float32)
        weight_matrix = lax.dynamic_slice_in_dim(mixing_weight_blocks, (owner * PMAX).astype(jnp.int32), PMAX, 0).astype(jnp.float32)
        partial_share = jnp.einsum('jny,jyb->jnb', selected_items, weight_matrix)
        partial_share = jnp.where(valid[:, None, None], partial_share, jnp.zeros_like(partial_share))
        wins = jax.ops.segment_sum(partial_share, window[owner], num_segments=nwin)
        tile = wins.reshape(ROWS // WIN_R, COLS // WIN_C, FEATS, WIN_R, WIN_C).transpose(2, 0, 3, 1, 4)
        return tile.reshape(FEATS, ROWS, COLS).astype(jnp.bfloat16)

    tiles = lax.map(one_tile, jnp.arange(ndev, dtype=jnp.int32))
    blended = tiles.reshape(N_NORTH, N_EAST, FEATS, ROWS, COLS).transpose(2, 0, 3, 1, 4)
    blended = blended.reshape(FEATS, N_NORTH * ROWS, N_EAST * COLS)
    half_r = N_NORTH * ROWS // 2
    half_c = N_EAST * COLS // 2
    patches = blended.reshape(FEATS, half_r, 2, half_c, 2).transpose(0, 2, 4, 1, 3).reshape(4 * FEATS, half_r * half_c)
    feats = jax.nn.gelu(jnp.dot(proj_weight, patches, preferred_element_type=jnp.float32))
    feats = feats.astype(jnp.bfloat16).reshape(CHANNELS, half_r, half_c)
    for layer in range(LAYERS):
        hidden = dilated_filter_layer(feats, conv_weight[layer], rates[layer])
        feats = (feats.astype(jnp.float32) + jax.nn.gelu(hidden)).astype(jnp.bfloat16)
    return feats
```

```python
import functools

import jax
import jax.numpy as jnp
from jax import lax
from jax.experimental import pallas as pl
from jax.experimental.pallas import tpu as pltpu
from jax.sharding import PartitionSpec as P

MESH = pl.DeviceIdType.MESH
NN, NE = 8, 16
ND = NN * NE
GATES = 128
FEATS = 16
CHANNELS = 64
LAYERS = 3
HALO = 4
HR, HC = 32, 128
PMAX = 256
BF, F32 = jnp.bfloat16, jnp.float32


def exchange_kernel(pick, gates, out, s0, s1, m0, m1, ssem, rsem):
    n, e = lax.axis_index("north"), lax.axis_index("east")
    bar = pltpu.get_barrier_semaphore()
    peers_e = [lax.rem(e + i, NE) for i in range(1, NE)]
    peers_n = [lax.rem(n + i, NN) for i in range(1, NN)]
    for te in peers_e:
        pl.semaphore_signal(bar, inc=1, device_id=(n, te), device_id_type=MESH)
    for tn in peers_n:
        pl.semaphore_signal(bar, inc=1, device_id=(tn, e), device_id_type=MESH)

    def gather(t, carry):
        tn, te = t // NE, lax.rem(t, NE)
        for k in range(2):
            p = pick[0, 2 * t + k]
            v = gates[jnp.maximum(p, 0)]
            v = jnp.where(p >= 0, v, jnp.zeros_like(v))
            if k == 0:
                s0[te, tn] = v
            else:
                s1[tn, te] = v
        return carry

    lax.fori_loop(0, ND, gather, 0, unroll=8)
    pl.semaphore_wait(bar, NE + NN - 2)
    f0, f1 = out.at[0], out.at[1]

    def remote(src, dst, k, dev):
        return pltpu.make_async_remote_copy(
            src_ref=src, dst_ref=dst, send_sem=ssem.at[k], recv_sem=rsem.at[k],
            device_id=dev, device_id_type=MESH,
        )

    for i in range(NE - 1):
        remote(s0.at[peers_e[i]], m0.at[e], 0, (n, peers_e[i])).start()
        if i < NN - 1:
            remote(s1.at[peers_n[i]], m1.at[n], 1, (peers_n[i], e)).start()
    m0[e] = s0[e]
    m1[n] = s1[n]

    def wait(ref, count, sem):
        r = ref.at[pl.ds(0, count)]
        pltpu.make_async_copy(r, r, sem).wait()

    wait(m1, NN - 1, rsem.at[1])
    for te in peers_e:
        remote(m1.at[:, te], f1.at[pl.ds(e * NN, NN)], 3, (n, te)).start()
    f1[pl.ds(e * NN, NN)] = m1[:, e]
    wait(m0, NE - 1, rsem.at[0])
    for tn in peers_n:
        remote(m0.at[:, tn], f0.at[pl.ds(n * NE, NE)], 2, (tn, e)).start()
    f0[pl.ds(n * NE, NE)] = m0[:, n]
    wait(f1, ND - NN, rsem.at[3])
    wait(f0, ND - NE, rsem.at[2])
    wait(m0, NE - 1, ssem.at[0])
    wait(m1, NN - 1, ssem.at[1])
    wait(f0, ND - NE, ssem.at[2])
    wait(f1, ND - NN, ssem.at[3])


def exchange(pick, gates):
    blk = (FEATS, GATES)
    return pl.pallas_call(
        exchange_kernel,
        out_shape=jax.ShapeDtypeStruct((2, ND) + blk, BF),
        in_specs=[pl.BlockSpec(memory_space=pltpu.SMEM), pl.BlockSpec(memory_space=pltpu.VMEM)],
        out_specs=pl.BlockSpec(memory_space=pltpu.VMEM),
        scratch_shapes=[
            pltpu.VMEM((NE, NN) + blk, BF), pltpu.VMEM((NN, NE) + blk, BF),
            pltpu.VMEM((NE, NN) + blk, BF), pltpu.VMEM((NN, NE) + blk, BF),
            pltpu.SemaphoreType.DMA((4,)), pltpu.SemaphoreType.DMA((4,)),
        ],
        compiler_params=pltpu.CompilerParams(
            collective_id=0, has_side_effects=True, vmem_limit_bytes=40 << 20),
        name="exchange",
    )(pick, gates)


NCH = 8
CH = PMAX // NCH


def iota(shape, dim):
    return lax.broadcasted_iota(jnp.int32, shape, dim)


def blend_kernel(feed_s, feed_v, win_v, rows, w_hbm, proj, x0, wbuf, share, grid, sem):
    for c in range(NCH):
        pltpu.make_async_copy(w_hbm.at[pl.ds(c * CH, CH)], wbuf.at[pl.ds(c * CH, CH)], sem.at[c]).start()
    hot = (win_v[...] == iota((GATES, PMAX), 0)) & (feed_v[...] >= 0)
    hot = jnp.where(hot, 1.0, 0.0).astype(BF)
    hot2 = jnp.concatenate([hot, hot], axis=1)

    def product(p, carry):
        j = jnp.maximum(feed_s[0, p], 0)
        s, k = j // 2, lax.rem(j, 2)
        q = jnp.where(k == 0, s, lax.rem(s, NE) * NN + s // NE)
        share[pl.ds(pl.multiple_of(p * FEATS, FEATS), FEATS), :] = jnp.dot(
            rows[k, q], wbuf[p], preferred_element_type=F32)
        return carry

    for c in range(NCH):
        pltpu.make_async_copy(w_hbm.at[pl.ds(c * CH, CH)], wbuf.at[pl.ds(c * CH, CH)], sem.at[c]).wait()
        lax.fori_loop(c * CH, c * CH + CH, product, 0, unroll=16)
    for f in range(0, FEATS, 2):
        parts = []
        for g in (f, f + 1):
            v = share[pl.ds(g, PMAX, stride=FEATS), :]
            hi = v.astype(BF)
            lo = (v - hi.astype(F32)).astype(BF)
            parts.append(jnp.concatenate([hi, lo], axis=0))
        r = jnp.dot(hot2, jnp.concatenate(parts, axis=1), preferred_element_type=F32)
        grid[pl.ds(f, 128, stride=FEATS), :] = r[:, :128]
        grid[pl.ds(f + 1, 128, stride=FEATS), :] = r[:, 128:]

    col = iota((1, 512), 1)
    i1, w1, a1, b1, j1 = col // 128, col // 32 % 4, col // 16 % 2, col // 8 % 2, col % 8
    src1 = w1 * 128 + i1 * 32 + a1 * 16 + j1 * 2 + b1
    t1 = jnp.where(iota((512, 512), 0) == src1, 1.0, 0.0).astype(BF)
    q2, wh2, wl2, j2 = col // 128, col // 32 % 4, col // 8 % 4, col % 8
    src2 = wh2 * 128 + wl2 * 32 + q2 * 8 + j2
    t2 = jnp.where(iota((512, 512), 0) == src2, 1.0, 0.0).astype(BF)
    tiles = []
    for wh in range(4):
        line = []
        for wl in range(4):
            wc = wh * 4 + wl
            blocks = [grid[pl.ds((wr * 16 + wc) * FEATS, FEATS), :] for wr in range(8)]
            line.append(jnp.concatenate(blocks, axis=0).astype(BF))
        tiles.append(jnp.concatenate(line, axis=1))
    y = jnp.dot(jnp.concatenate(tiles, axis=0), t1, preferred_element_type=F32).astype(BF)
    tiles = [
        jnp.concatenate([y[wh * 128:(wh + 1) * 128, i * 128:(i + 1) * 128] for wh in range(4)], axis=1)
        for i in range(4)
    ]
    z = jnp.dot(jnp.concatenate(tiles, axis=0), t2, preferred_element_type=F32).astype(BF)
    for wr in range(8):
        cells = []
        for i in range(4):
            r0 = (i * 8 + wr) * FEATS
            cells.append(jnp.concatenate(
                [z[r0:r0 + FEATS, q * 128:(q + 1) * 128] for q in range(4)], axis=0))
        o = jnp.dot(proj[...], jnp.concatenate(cells, axis=1), preferred_element_type=F32)
        o = jax.nn.gelu(o).astype(BF)
        for i in range(4):
            x0[wr * 4 + i] = o[:, i * 128:(i + 1) * 128]


def blend(feed, window, rows, w, proj):
    vm = pl.BlockSpec(memory_space=pltpu.VMEM)
    return pl.pallas_call(
        blend_kernel,
        out_shape=jax.ShapeDtypeStruct((HR, CHANNELS, HC), BF),
        in_specs=[pl.BlockSpec(memory_space=pltpu.SMEM), vm, vm, vm, pl.BlockSpec(memory_space=pl.ANY), vm],
        out_specs=vm,
        scratch_shapes=[
            pltpu.VMEM((PMAX, GATES, 128), BF),
            pltpu.VMEM((PMAX * FEATS, 128), F32),
            pltpu.VMEM((128 * FEATS, 128), F32),
            pltpu.SemaphoreType.DMA((NCH,)),
        ],
        compiler_params=pltpu.CompilerParams(vmem_limit_bytes=40 << 20),
        name="blend",
    )(feed, feed, window, rows, w, proj)


ER = HR + 2 * HALO


def conv_kernel(rates, x0, wall, out, ext, edges, halo, ybuf, fbuf, ssem, rsem):
    n, e = lax.axis_index("north"), lax.axis_index("east")
    up, down = lax.rem(n + NN - 1, NN), lax.rem(n + 1, NN)
    left, right = lax.rem(e + NE - 1, NE), lax.rem(e + 1, NE)
    bar = pltpu.get_barrier_semaphore()
    for tn in (up, n, down):
        for te in (left, e, right):
            if tn is n and te is e:
                continue
            pl.semaphore_signal(bar, inc=1, device_id=(tn, te), device_id_type=MESH)
    lane = iota((CHANNELS, HC), 1)
    row_ok = [(n > 0), None, (n < NN - 1)]
    col_ok = [(e > 0), (e < NE - 1)]

    def pack(layer, get):
        el = jnp.zeros((CHANNELS, HC), F32)
        er = jnp.zeros((CHANNELS, HC), F32)
        for r in range(HR):
            v = get(r)
            here = (lane // HALO) == r
            el = jnp.where(here, pltpu.roll(v, 4 * r, 1) if r else v, el)
            er = jnp.where(here, pltpu.roll(v, (4 * r + 4) % 128, 1) if r < HR - 1 else v, er)
        edges[layer, 0] = el.astype(BF)
        edges[layer, 1] = er.astype(BF)

    def load(i, carry):
        ext[0, i + HALO] = x0[i]
        fbuf[pl.ds(pl.multiple_of(i * CHANNELS, CHANNELS), CHANNELS), :] = x0[i].astype(F32)
        return carry

    lax.fori_loop(0, HR, load, 0, unroll=8)

    for layer in range(LAYERS):
        pack(layer, lambda r: fbuf[r * CHANNELS:(r + 1) * CHANNELS, :])
        if layer == 0:
            pl.semaphore_wait(bar, 8)

        def remote(src, dst, dev):
            cp = pltpu.make_async_remote_copy(
                src_ref=src, dst_ref=dst, send_sem=ssem.at[layer], recv_sem=rsem.at[layer],
                device_id=dev, device_id_type=MESH)
            cp.start()

        remote(ext.at[layer, pl.ds(HALO, HALO)], ext.at[layer, pl.ds(HALO + HR, HALO)], (up, e))
        remote(ext.at[layer, pl.ds(HR, HALO)], ext.at[layer, pl.ds(0, HALO)], (down, e))
        for k, tn in ((2, up), (1, n), (0, down)):
            remote(edges.at[layer, 1], halo.at[layer, k], (tn, right))
            remote(edges.at[layer, 0], halo.at[layer, 3 + k], (tn, left))
        everything = ext.at[layer, pl.ds(0, 14)]
        pltpu.make_async_copy(everything, everything, rsem.at[layer]).wait()

        d = rates[layer]
        w = wall[layer]

        def one_row(m, k, rr):
            x = ext[layer, m].astype(F32)
            lt = halo[layer, k].astype(F32)
            rt = halo[layer, 3 + k].astype(F32)
            ok = row_ok[k]
            if ok is not None:
                x = jnp.where(ok, x, 0.0)
            okl = col_ok[0] if ok is None else jnp.logical_and(ok, col_ok[0])
            okr = col_ok[1] if ok is None else jnp.logical_and(ok, col_ok[1])
            lt = jnp.where(okl, lt, 0.0)
            rt = jnp.where(okr, rt, 0.0)
            lt = pltpu.roll(lt, lax.rem(d + 124 - 4 * rr + 128, 128), 1)
            xl = jnp.where(lane >= d, pltpu.roll(x, d, 1), lt)
            rt = pltpu.roll(rt, lax.rem(256 - d - 4 * rr, 128), 1)
            xr = jnp.where(lane < HC - d, pltpu.roll(x, HC - d, 1), rt)
            return jnp.concatenate([xl.astype(BF), x.astype(BF), xr.astype(BF)], axis=0)

        def two_rows(m, k, rr):
            b = jnp.concatenate([one_row(m, k, rr), one_row(m + 1, k, rr + 1)], axis=1)
            y = jnp.dot(w, b, preferred_element_type=F32)
            ybuf[m] = y[:, :HC]
            ybuf[m + 1] = y[:, HC:]

        for m in (0, 2):
            two_rows(m, 0, HR - HALO + m)
        lax.fori_loop(0, HR // 2, lambda i, c: (two_rows(HALO + 2 * i, 1, 2 * i), c)[1], 0, unroll=4)
        for m in (0, 2):
            two_rows(HALO + HR + m, 2, m)

        def finish(i, carry):
            h = (ybuf[i + HALO - d, 0:64, :] + ybuf[i + HALO, 64:128, :]
                 + ybuf[i + HALO + d, 128:192, :])
            at = pl.ds(pl.multiple_of(i * CHANNELS, CHANNELS), CHANNELS)
            v = (fbuf[at, :] + jax.nn.gelu(h)).astype(BF)
            fbuf[at, :] = v.astype(F32)
            if layer < LAYERS - 1:
                ext[layer + 1, i + HALO] = v
            return carry

        lax.fori_loop(0, HR, finish, 0, unroll=4)

    for c in range(CHANNELS):
        out[c] = fbuf[pl.ds(c, HR, stride=CHANNELS), :].astype(BF)
    for layer in range(LAYERS):
        everything = ext.at[layer, pl.ds(0, 14)]
        pltpu.make_async_copy(everything, everything, ssem.at[layer]).wait()


def conv(rates, x0, wall):
    vm = pl.BlockSpec(memory_space=pltpu.VMEM)
    return pl.pallas_call(
        conv_kernel,
        out_shape=jax.ShapeDtypeStruct((CHANNELS, HR, HC), BF),
        in_specs=[pl.BlockSpec(memory_space=pltpu.SMEM), vm, vm],
        out_specs=vm,
        scratch_shapes=[
            pltpu.VMEM((LAYERS, ER, CHANNELS, HC), BF),
            pltpu.VMEM((LAYERS, 2, CHANNELS, HC), BF),
            pltpu.VMEM((LAYERS, 6, CHANNELS, HC), BF),
            pltpu.VMEM((ER, 3 * CHANNELS, HC), F32),
            pltpu.VMEM((HR * CHANNELS, HC), F32),
            pltpu.SemaphoreType.DMA((LAYERS,)), pltpu.SemaphoreType.DMA((LAYERS,)),
        ],
        compiler_params=pltpu.CompilerParams(
            collective_id=1, has_side_effects=True, vmem_limit_bytes=40 << 20),
        name="conv",
    )(rates, x0, wall)


def per_device(gates, mixing_weight_blocks, send_pick, feed, window, proj_weight, conv_weight, rates):
    rows = exchange(send_pick.reshape(1, 2 * ND), gates)
    proj = proj_weight.reshape(CHANNELS, FEATS, 4).transpose(0, 2, 1).reshape(CHANNELS, 4 * FEATS)
    x0 = blend(feed, window, rows, mixing_weight_blocks, proj)
    wall = conv_weight.reshape(LAYERS, 3, 3, CHANNELS, CHANNELS).transpose(0, 1, 3, 2, 4)
    wall = wall.reshape(LAYERS, 3 * CHANNELS, 3 * CHANNELS)
    return conv(rates, x0, wall)


def solution(mesh):
    in_specs = (
        P(("north", "east"), None, None),
        P(("north", "east"), None, None),
        P(("north", "east"), None, None),
        P(("north", "east"), None),
        P(("north", "east"), None),
        P(),
        P(),
        P(),
    )
    return jax.shard_map(
        per_device, mesh=mesh, in_specs=in_specs, out_specs=P(None, "north", "east"), check_vma=False
    )
```

```python
import functools

import jax
import jax.numpy as jnp
from jax import lax
from jax.experimental import pallas as pl
from jax.experimental.pallas import tpu as pltpu
from jax.sharding import PartitionSpec as P

MESH = pl.DeviceIdType.MESH
NN, NE = 8, 16
ND = NN * NE
GATES = 128
FEATS = 16
CHANNELS = 64
LAYERS = 3
HALO = 4
HR, HC = 32, 128
PMAX = 256
BF, F32 = jnp.bfloat16, jnp.float32


NCH = 8
CH = PMAX // NCH
ER = HR + 2 * HALO


def iota(shape, dim):
    return lax.broadcasted_iota(jnp.int32, shape, dim)


def places():
    n, e = lax.axis_index("north"), lax.axis_index("east")
    up, down = lax.rem(n + NN - 1, NN), lax.rem(n + 1, NN)
    left, right = lax.rem(e + NE - 1, NE), lax.rem(e + 1, NE)
    return n, e, up, down, left, right


def exchange(pick, gates, s0, s1, m0, m1, rows, ssem, rsem, bar, meanwhile):
    n, e, up, down, left, right = places()
    peers_e = [lax.rem(e + i, NE) for i in range(1, NE)]
    peers_n = [lax.rem(n + i, NN) for i in range(1, NN)]

    def gather(t, carry):
        tn, te = t // NE, lax.rem(t, NE)
        for k in range(2):
            p = pick[0, k, t]
            v = gates[jnp.maximum(p, 0)]
            v = jnp.where(p >= 0, v, jnp.zeros_like(v))
            if k == 0:
                s0[te, tn] = v
            else:
                s1[tn, te] = v
        return carry

    lax.fori_loop(0, ND, gather, 0, unroll=8)
    pl.semaphore_wait(bar, NE + NN - 2 + 4)
    f0, f1 = rows.at[0], rows.at[1]

    def remote(src, dst, k, dev):
        return pltpu.make_async_remote_copy(
            src_ref=src, dst_ref=dst, send_sem=ssem.at[k], recv_sem=rsem.at[k],
            device_id=dev, device_id_type=MESH,
        )

    for i in range(NE - 1):
        remote(s0.at[peers_e[i]], m0.at[e], 0, (n, peers_e[i])).start()
        if i < NN - 1:
            remote(s1.at[peers_n[i]], m1.at[n], 1, (peers_n[i], e)).start()
    m0[e] = s0[e]
    m1[n] = s1[n]
    meanwhile()

    def wait(ref, count, sem):
        r = ref.at[pl.ds(0, count)]
        pltpu.make_async_copy(r, r, sem).wait()

    wait(m1, NN - 1, rsem.at[1])
    for te in peers_e:
        remote(m1.at[:, te], f1.at[pl.ds(e * NN, NN)], 3, (n, te)).start()
    f1[pl.ds(e * NN, NN)] = m1[:, e]
    wait(m0, NE - 1, rsem.at[0])
    for tn in peers_n:
        remote(m0.at[:, tn], f0.at[pl.ds(n * NE, NE)], 2, (tn, e)).start()
    f0[pl.ds(n * NE, NE)] = m0[:, n]
    wait(f1, ND - NN, rsem.at[3])
    wait(f0, ND - NE, rsem.at[2])

    def sent():
        wait(m0, NE - 1, ssem.at[0])
        wait(m1, NN - 1, ssem.at[1])
        wait(f0, ND - NE, ssem.at[2])
        wait(f1, ND - NN, ssem.at[3])

    return sent


def tables(win_v, feed_v, proj, taps, hot2, t1, t2, projq, wall):
    hot = (win_v[...] == iota((GATES, PMAX), 0)) & (feed_v[...] >= 0)
    hot = jnp.where(hot, 1.0, 0.0).astype(BF)
    hot2[...] = jnp.concatenate([hot, hot], axis=1)
    col = iota((1, 512), 1)
    i1, w1, a1, b1, j1 = col // 128, col // 32 % 4, col // 16 % 2, col // 8 % 2, col % 8
    src1 = w1 * 128 + i1 * 32 + a1 * 16 + j1 * 2 + b1
    t1[...] = jnp.where(iota((512, 512), 0) == src1, 1.0, 0.0).astype(BF)
    q2, wh2, wl2, j2 = col // 128, col // 32 % 4, col // 8 % 4, col % 8
    src2 = wh2 * 128 + wl2 * 32 + q2 * 8 + j2
    t2[...] = jnp.where(iota((512, 512), 0) == src2, 1.0, 0.0).astype(BF)
    c = iota((1, 64), 1)
    p = jnp.where(iota((64, 64), 0) == c % 16 * 4 + c // 16, 1.0, 0.0).astype(BF)
    projq[...] = jnp.dot(proj[...], p, preferred_element_type=F32).astype(BF)
    for layer in range(LAYERS):
        for a in range(3):
            line = [taps[layer, a * 3 + b].astype(F32) for b in range(3)]
            wall[layer, a * CHANNELS:(a + 1) * CHANNELS, :] = jnp.concatenate(line, axis=1).astype(BF)


def blend(feed_s, rows, wbuf, share, grid, hot2, t1, t2, projq, wait_w, put):
    def product(p, carry):
        j = jnp.maximum(feed_s[0, p], 0)
        s, k = j // 2, lax.rem(j, 2)
        q = jnp.where(k == 0, s, lax.rem(s, NE) * NN + s // NE)
        share[pl.ds(pl.multiple_of(p * FEATS, FEATS), FEATS), :] = jnp.dot(
            rows[k, q], wbuf[p], preferred_element_type=F32)
        return carry

    wait_w()
    lax.fori_loop(0, PMAX, product, 0, unroll=16)
    for f in range(0, FEATS, 2):
        parts = []
        for g in (f, f + 1):
            v = share[pl.ds(g, PMAX, stride=FEATS), :]
            hi = v.astype(BF)
            lo = (v - hi.astype(F32)).astype(BF)
            parts.append(jnp.concatenate([hi, lo], axis=0))
        r = jnp.dot(hot2[...], jnp.concatenate(parts, axis=1), preferred_element_type=F32)
        grid[pl.ds(f, 128, stride=FEATS), :] = r[:, :128]
        grid[pl.ds(f + 1, 128, stride=FEATS), :] = r[:, 128:]

    tiles = []
    for wh in range(4):
        line = []
        for wl in range(4):
            wc = wh * 4 + wl
            blocks = [grid[pl.ds((wr * 16 + wc) * FEATS, FEATS), :] for wr in range(8)]
            line.append(jnp.concatenate(blocks, axis=0).astype(BF))
        tiles.append(jnp.concatenate(line, axis=1))
    y = jnp.dot(jnp.concatenate(tiles, axis=0), t1[...], preferred_element_type=F32).astype(BF)
    tiles = [
        jnp.concatenate([y[wh * 128:(wh + 1) * 128, i * 128:(i + 1) * 128] for wh in range(4)], axis=1)
        for i in range(4)
    ]
    z = jnp.dot(jnp.concatenate(tiles, axis=0), t2[...], preferred_element_type=F32).astype(BF)
    for wr in range(8):
        cells = []
        for i in range(4):
            r0 = (i * 8 + wr) * FEATS
            cells.append(jnp.concatenate(
                [z[r0:r0 + FEATS, q * 128:(q + 1) * 128] for q in range(4)], axis=0))
        o = jnp.dot(projq[...], jnp.concatenate(cells, axis=1), preferred_element_type=F32)
        o = jax.nn.gelu(o).astype(BF)
        for i in range(4):
            put(wr * 4 + i, o[:, i * 128:(i + 1) * 128])


def conv(rates, wall, out, ext, edges, halo, ybuf, fbuf, ssem, rsem):
    n, e, up, down, left, right = places()
    lane = iota((CHANNELS, HC), 1)
    row_ok = [(n > 0), None, (n < NN - 1)]
    col_ok = [(e > 0), (e < NE - 1)]

    def pack(layer, get):
        el = jnp.zeros((CHANNELS, HC), F32)
        er = jnp.zeros((CHANNELS, HC), F32)
        for r in range(HR):
            v = get(r)
            here = (lane // HALO) == r
            el = jnp.where(here, pltpu.roll(v, 4 * r, 1) if r else v, el)
            er = jnp.where(here, pltpu.roll(v, (4 * r + 4) % 128, 1) if r < HR - 1 else v, er)
        edges[layer, 0] = el.astype(BF)
        edges[layer, 1] = er.astype(BF)

    for layer in range(LAYERS):
        pack(layer, lambda r: fbuf[r * CHANNELS:(r + 1) * CHANNELS, :])

        def remote(src, dst, dev):
            cp = pltpu.make_async_remote_copy(
                src_ref=src, dst_ref=dst, send_sem=ssem.at[layer], recv_sem=rsem.at[layer],
                device_id=dev, device_id_type=MESH)
            cp.start()

        remote(ext.at[layer, pl.ds(HALO, HALO)], ext.at[layer, pl.ds(HALO + HR, HALO)], (up, e))
        remote(ext.at[layer, pl.ds(HR, HALO)], ext.at[layer, pl.ds(0, HALO)], (down, e))
        for k, tn in ((2, up), (1, n), (0, down)):
            remote(edges.at[layer, 1], halo.at[layer, k], (tn, right))
            remote(edges.at[layer, 0], halo.at[layer, 3 + k], (tn, left))
        everything = ext.at[layer, pl.ds(0, 14)]
        pltpu.make_async_copy(everything, everything, rsem.at[layer]).wait()

        d = rates[layer]
        w = wall[layer]

        def one_row(m, k, rr):
            x = ext[layer, m].astype(F32)
            lt = halo[layer, k].astype(F32)
            rt = halo[layer, 3 + k].astype(F32)
            ok = row_ok[k]
            if ok is not None:
                x = jnp.where(ok, x, 0.0)
            okl = col_ok[0] if ok is None else jnp.logical_and(ok, col_ok[0])
            okr = col_ok[1] if ok is None else jnp.logical_and(ok, col_ok[1])
            lt = jnp.where(okl, lt, 0.0)
            rt = jnp.where(okr, rt, 0.0)
            lt = pltpu.roll(lt, lax.rem(d + 124 - 4 * rr + 128, 128), 1)
            xl = jnp.where(lane >= d, pltpu.roll(x, d, 1), lt)
            rt = pltpu.roll(rt, lax.rem(256 - d - 4 * rr, 128), 1)
            xr = jnp.where(lane < HC - d, pltpu.roll(x, HC - d, 1), rt)
            return jnp.concatenate([xl.astype(BF), x.astype(BF), xr.astype(BF)], axis=0)

        def two_rows(m, k, rr):
            b = jnp.concatenate([one_row(m, k, rr), one_row(m + 1, k, rr + 1)], axis=1)
            y = jnp.dot(w, b, preferred_element_type=F32)
            ybuf[m] = y[:, :HC]
            ybuf[m + 1] = y[:, HC:]

        for m in (0, 2):
            two_rows(m, 0, HR - HALO + m)
        lax.fori_loop(0, HR // 2, lambda i, c: (two_rows(HALO + 2 * i, 1, 2 * i), c)[1], 0, unroll=4)
        for m in (0, 2):
            two_rows(HALO + HR + m, 2, m)

        def finish(i, carry):
            h = (ybuf[i + HALO - d, 0:64, :] + ybuf[i + HALO, 64:128, :]
                 + ybuf[i + HALO + d, 128:192, :])
            at = pl.ds(pl.multiple_of(i * CHANNELS, CHANNELS), CHANNELS)
            v = (fbuf[at, :] + jax.nn.gelu(h)).astype(BF)
            fbuf[at, :] = v.astype(F32)
            if layer < LAYERS - 1:
                ext[layer + 1, i + HALO] = v
            return carry

        lax.fori_loop(0, HR, finish, 0, unroll=4)

    for c in range(CHANNELS):
        out[c] = fbuf[pl.ds(c, HR, stride=CHANNELS), :].astype(BF)
    for layer in range(LAYERS):
        everything = ext.at[layer, pl.ds(0, 14)]
        pltpu.make_async_copy(everything, everything, ssem.at[layer]).wait()


def kernel(pick, feed_s, rates, feed_v, win_v, gates_hbm, w_hbm, proj, taps, out,
           s0, s1, m0, m1, rows, gates, wbuf, share, grid, hot2, t1, t2, projq, wall,
           ext, edges, halo, ybuf, fbuf, asem, arem, ssem, rsem, lsem):
    n, e, up, down, left, right = places()
    load_g = pltpu.make_async_copy(gates_hbm, gates, lsem.at[0])
    load_g.start()
    load_w = pltpu.make_async_copy(w_hbm, wbuf, lsem.at[1])
    load_w.start()
    bar = pltpu.get_barrier_semaphore()
    for i in range(1, NE):
        pl.semaphore_signal(bar, inc=1, device_id=(n, lax.rem(e + i, NE)), device_id_type=MESH)
    for i in range(1, NN):
        pl.semaphore_signal(bar, inc=1, device_id=(lax.rem(n + i, NN), e), device_id_type=MESH)
    for tn in (up, down):
        for te in (left, right):
            pl.semaphore_signal(bar, inc=1, device_id=(tn, te), device_id_type=MESH)
    load_g.wait()
    sent = exchange(pick, gates, s0, s1, m0, m1, rows, asem, arem, bar,
                    lambda: tables(win_v, feed_v, proj, taps, hot2, t1, t2, projq, wall))

    def put(i, v):
        ext[0, i + HALO] = v
        fbuf[i * CHANNELS:(i + 1) * CHANNELS, :] = v.astype(F32)

    blend(feed_s, rows, wbuf, share, grid, hot2, t1, t2, projq, load_w.wait, put)
    conv(rates, wall, out, ext, edges, halo, ybuf, fbuf, ssem, rsem)
    sent()


def per_device(gates, mixing_weight_blocks, send_pick, feed, window, proj_weight, conv_weight, rates):
    vm, sm = pl.BlockSpec(memory_space=pltpu.VMEM), pl.BlockSpec(memory_space=pltpu.SMEM)
    hbm = pl.BlockSpec(memory_space=pl.ANY)
    blk = (FEATS, GATES)
    return pl.pallas_call(
        kernel,
        out_shape=jax.ShapeDtypeStruct((CHANNELS, HR, HC), BF),
        in_specs=[sm, sm, sm, vm, vm, hbm, hbm, vm, vm],
        out_specs=vm,
        scratch_shapes=[
            pltpu.VMEM((NE, NN) + blk, BF), pltpu.VMEM((NN, NE) + blk, BF),
            pltpu.VMEM((NE, NN) + blk, BF), pltpu.VMEM((NN, NE) + blk, BF),
            pltpu.VMEM((2, ND) + blk, BF), pltpu.VMEM((PMAX,) + blk, BF),
            pltpu.VMEM((PMAX, GATES, 128), BF),
            pltpu.VMEM((PMAX * FEATS, 128), F32),
            pltpu.VMEM((128 * FEATS, 128), F32),
            pltpu.VMEM((128, 512), BF), pltpu.VMEM((512, 512), BF), pltpu.VMEM((512, 512), BF),
            pltpu.VMEM((CHANNELS, 64), BF), pltpu.VMEM((LAYERS, 3 * CHANNELS, 3 * CHANNELS), BF),
            pltpu.VMEM((LAYERS, ER, CHANNELS, HC), BF),
            pltpu.VMEM((LAYERS, 2, CHANNELS, HC), BF),
            pltpu.VMEM((LAYERS, 6, CHANNELS, HC), BF),
            pltpu.VMEM((ER, 3 * CHANNELS, HC), F32),
            pltpu.VMEM((HR * CHANNELS, HC), F32),
            pltpu.SemaphoreType.DMA((4,)), pltpu.SemaphoreType.DMA((4,)),
            pltpu.SemaphoreType.DMA((LAYERS,)), pltpu.SemaphoreType.DMA((LAYERS,)),
            pltpu.SemaphoreType.DMA((2,)),
        ],
        compiler_params=pltpu.CompilerParams(
            collective_id=0, has_side_effects=True, vmem_limit_bytes=58 << 20),
        name="radar",
    )(send_pick.transpose(0, 2, 1), feed, rates, feed, window, gates, mixing_weight_blocks, proj_weight, conv_weight)


def solution(mesh):
    in_specs = (
        P(("north", "east"), None, None),
        P(("north", "east"), None, None),
        P(("north", "east"), None, None),
        P(("north", "east"), None),
        P(("north", "east"), None),
        P(),
        P(),
        P(),
    )
    return jax.shard_map(
        per_device, mesh=mesh, in_specs=in_specs, out_specs=P(None, "north", "east"), check_vma=False
    )
```

```python
import functools

import jax
import jax.numpy as jnp
from jax import lax
from jax.experimental import pallas as pl
from jax.experimental.pallas import tpu as pltpu
from jax.sharding import PartitionSpec as P

MESH = pl.DeviceIdType.MESH
NN, NE = 8, 16
ND = NN * NE
GATES = 128
FEATS = 16
CHANNELS = 64
LAYERS = 3
HALO = 4
HR, HC = 32, 128
PMAX = 256
BF, F32 = jnp.bfloat16, jnp.float32


NCH = 8
CH = PMAX // NCH
REACH = LAYERS * HALO
ROWS = HR + 2 * REACH
TILES, OFF, SPLIT = 36, 20, 28


def iota(shape, dim):
    return lax.broadcasted_iota(jnp.int32, shape, dim)


def places():
    n, e = lax.axis_index("north"), lax.axis_index("east")
    up, down = lax.rem(n + NN - 1, NN), lax.rem(n + 1, NN)
    left, right = lax.rem(e + NE - 1, NE), lax.rem(e + 1, NE)
    return n, e, up, down, left, right


def exchange(pick, gates, s0, s1, m0, m1, rows, ssem, rsem, bar, meanwhile):
    n, e, up, down, left, right = places()
    peers_e = [lax.rem(e + i, NE) for i in range(1, NE)]
    peers_n = [lax.rem(n + i, NN) for i in range(1, NN)]

    def gather(t, carry):
        tn, te = t // NE, lax.rem(t, NE)
        for k in range(2):
            p = pick[0, k, t]
            v = gates[jnp.maximum(p, 0)]
            v = jnp.where(p >= 0, v, jnp.zeros_like(v))
            if k == 0:
                s0[te, tn] = v
            else:
                s1[tn, te] = v
        return carry

    lax.fori_loop(0, ND, gather, 0, unroll=8)
    pl.semaphore_wait(bar, NE + NN - 2 + 4)
    f0, f1 = rows.at[0], rows.at[1]

    def remote(src, dst, k, dev):
        return pltpu.make_async_remote_copy(
            src_ref=src, dst_ref=dst, send_sem=ssem.at[k], recv_sem=rsem.at[k],
            device_id=dev, device_id_type=MESH,
        )

    for i in range(NE - 1):
        remote(s0.at[peers_e[i]], m0.at[e], 0, (n, peers_e[i])).start()
        if i < NN - 1:
            remote(s1.at[peers_n[i]], m1.at[n], 1, (peers_n[i], e)).start()
    m0[e] = s0[e]
    m1[n] = s1[n]
    meanwhile()

    def wait(ref, count, sem):
        r = ref.at[pl.ds(0, count)]
        pltpu.make_async_copy(r, r, sem).wait()

    wait(m1, NN - 1, rsem.at[1])
    for te in peers_e:
        remote(m1.at[:, te], f1.at[pl.ds(e * NN, NN)], 3, (n, te)).start()
    f1[pl.ds(e * NN, NN)] = m1[:, e]
    wait(m0, NE - 1, rsem.at[0])
    for tn in peers_n:
        remote(m0.at[:, tn], f0.at[pl.ds(n * NE, NE)], 2, (tn, e)).start()
    f0[pl.ds(n * NE, NE)] = m0[:, n]
    wait(f1, ND - NN, rsem.at[3])
    wait(f0, ND - NE, rsem.at[2])

    def sent():
        wait(m0, NE - 1, ssem.at[0])
        wait(m1, NN - 1, ssem.at[1])
        wait(f0, ND - NE, ssem.at[2])
        wait(f1, ND - NN, ssem.at[3])

    return sent


def tables(win_v, feed_v, proj, taps, hot2, t1, t2, projq, wall):
    hot = (win_v[...] == iota((GATES, PMAX), 0)) & (feed_v[...] >= 0)
    hot = jnp.where(hot, 1.0, 0.0).astype(BF)
    hot2[...] = jnp.concatenate([hot, hot], axis=1)
    col = iota((1, 512), 1)
    i1, w1, a1, b1, j1 = col // 128, col // 32 % 4, col // 16 % 2, col // 8 % 2, col % 8
    src1 = w1 * 128 + i1 * 32 + a1 * 16 + j1 * 2 + b1
    t1[...] = jnp.where(iota((512, 512), 0) == src1, 1.0, 0.0).astype(BF)
    q2, wh2, wl2, j2 = col // 128, col // 32 % 4, col // 8 % 4, col % 8
    src2 = wh2 * 128 + wl2 * 32 + q2 * 8 + j2
    t2[...] = jnp.where(iota((512, 512), 0) == src2, 1.0, 0.0).astype(BF)
    c = iota((1, 64), 1)
    p = jnp.where(iota((64, 64), 0) == c % 16 * 4 + c // 16, 1.0, 0.0).astype(BF)
    projq[...] = jnp.dot(proj[...], p, preferred_element_type=F32).astype(BF)
    for layer in range(LAYERS):
        for a in range(3):
            line = [taps[layer, a * 3 + b].astype(F32) for b in range(3)]
            wall[layer, a * CHANNELS:(a + 1) * CHANNELS, :] = jnp.concatenate(line, axis=1).astype(BF)


def blend(feed_s, rows, wbuf, share, grid, hot2, t1, t2, projq, wait_w, put):
    def product(p, carry):
        j = jnp.maximum(feed_s[0, p], 0)
        s, k = j // 2, lax.rem(j, 2)
        q = jnp.where(k == 0, s, lax.rem(s, NE) * NN + s // NE)
        share[pl.ds(pl.multiple_of(p * FEATS, FEATS), FEATS), :] = jnp.dot(
            rows[k, q], wbuf[p], preferred_element_type=F32)
        return carry

    wait_w()
    lax.fori_loop(0, PMAX, product, 0, unroll=64)
    for f in range(0, FEATS, 2):
        parts = []
        for g in (f, f + 1):
            v = share[pl.ds(g, PMAX, stride=FEATS), :]
            hi = v.astype(BF)
            lo = (v - hi.astype(F32)).astype(BF)
            parts.append(jnp.concatenate([hi, lo], axis=0))
        r = jnp.dot(hot2[...], jnp.concatenate(parts, axis=1), preferred_element_type=F32)
        grid[pl.ds(f, 128, stride=FEATS), :] = r[:, :128]
        grid[pl.ds(f + 1, 128, stride=FEATS), :] = r[:, 128:]

    tiles = []
    for wh in range(4):
        line = []
        for wl in range(4):
            wc = wh * 4 + wl
            blocks = [grid[pl.ds((wr * 16 + wc) * FEATS, FEATS), :] for wr in range(8)]
            line.append(jnp.concatenate(blocks, axis=0).astype(BF))
        tiles.append(jnp.concatenate(line, axis=1))
    y = jnp.dot(jnp.concatenate(tiles, axis=0), t1[...], preferred_element_type=F32).astype(BF)
    tiles = [
        jnp.concatenate([y[wh * 128:(wh + 1) * 128, i * 128:(i + 1) * 128] for wh in range(4)], axis=1)
        for i in range(4)
    ]
    z = jnp.dot(jnp.concatenate(tiles, axis=0), t2[...], preferred_element_type=F32).astype(BF)
    for wr in range(8):
        cells = []
        for i in range(4):
            r0 = (i * 8 + wr) * FEATS
            cells.append(jnp.concatenate(
                [z[r0:r0 + FEATS, q * 128:(q + 1) * 128] for q in range(4)], axis=0))
        o = jnp.dot(projq[...], jnp.concatenate(cells, axis=1), preferred_element_type=F32)
        o = jax.nn.gelu(o).astype(BF)
        for i in range(4):
            put(wr * 4 + i, o[:, i * 128:(i + 1) * 128])


def conv(rates, wall, out, xs, es, strips, halo, ybuf, ye, fbuf, ssem, rsem):
    n, e, up, down, left, right = places()
    lane = iota((CHANNELS, HC), 1)
    row_lane = iota((1, HC), 1)
    zero = jnp.zeros((CHANNELS, HC), BF)

    def remote(src, dst, dev):
        pltpu.make_async_remote_copy(
            src_ref=src, dst_ref=dst, send_sem=ssem.at[0], recv_sem=rsem.at[0],
            device_id=dev, device_id_type=MESH).start()

    for g in range(HR // 8):
        sl, sr = zero, zero
        for k in range(8):
            v = xs[0, REACH + 8 * g + k]
            here = lane // 16 == k
            sl = jnp.where(here, pltpu.roll(v, 16 * k, 1) if k else v, sl)
            sr = jnp.where(here, pltpu.roll(v, (16 * k + 16) % HC, 1) if k < 7 else v, sr)
        strips[0, g] = sl
        strips[1, g] = sr
    for side, te in ((0, right), (1, left)):
        own = strips.at[1 - side]
        remote(own, halo.at[side, pl.ds(2, 4)], (n, te))
        remote(own.at[pl.ds(2, 2)], halo.at[side, pl.ds(0, 2)], (down, te))
        remote(own.at[pl.ds(0, 2)], halo.at[side, pl.ds(6, 2)], (up, te))
    remote(xs.at[0, pl.ds(REACH, REACH)], xs.at[0, pl.ds(REACH + HR, REACH)], (up, e))
    remote(xs.at[0, pl.ds(HR, REACH)], xs.at[0, pl.ds(0, REACH)], (down, e))
    arrived = xs.at[0, pl.ds(0, 2 * REACH + 16)]
    pltpu.make_async_copy(arrived, arrived, rsem.at[0]).wait()

    @pl.when(n == 0)
    def _():
        xs[0, pl.ds(0, REACH)] = jnp.zeros((REACH, CHANNELS, HC), BF)

    @pl.when(n == NN - 1)
    def _():
        xs[0, pl.ds(REACH + HR, REACH)] = jnp.zeros((REACH, CHANNELS, HC), BF)

    up_ok, down_ok = jnp.where(n > 0, 1.0, 0.0), jnp.where(n < NN - 1, 1.0, 0.0)
    left_ok, right_ok = jnp.where(e > 0, 1.0, 0.0), jnp.where(e < NE - 1, 1.0, 0.0)
    part = row_lane % 64
    cols = jnp.where(part < 16, left_ok, jnp.where(part >= 48, right_ok, 1.0))

    def edge_mask(t):
        first = jnp.where(t < REACH, up_ok, 1.0)
        second = jnp.where(t + OFF >= REACH + HR, down_ok, 1.0)
        return cols * jnp.where(row_lane < 64, first, second)

    def assemble(t, carry):
        h0, o0 = (t + 4) // 8, lax.rem(t + 4, 8)
        h1, o1 = (t + OFF + 4) // 8, lax.rem(t + OFF + 4, 8)
        a, b = xs[0, t], xs[0, t + OFF]
        pieces = [
            pltpu.roll(halo[0, h0], lax.rem(HC - 16 * o0, HC), 1), pltpu.roll(a, 16, 1),
            pltpu.roll(a, 48, 1), pltpu.roll(halo[1, h0], lax.rem(HC + 48 - 16 * o0, HC), 1),
            pltpu.roll(halo[0, h1], lax.rem(HC + 64 - 16 * o1, HC), 1), pltpu.roll(b, 80, 1),
            pltpu.roll(b, 112, 1), pltpu.roll(halo[1, h1], lax.rem(HC + 112 - 16 * o1, HC), 1),
        ]
        v = pieces[0]
        for k in range(1, 8):
            v = jnp.where(lane // 16 == k, pieces[k], v)
        es[0, t] = (v.astype(F32) * edge_mask(t)).astype(BF)
        return carry

    lax.fori_loop(0, TILES, assemble, 0, unroll=12)

    for layer in range(LAYERS):
        d = rates[layer]
        w = wall[layer]
        lo = HALO * layer

        def one_row(m, second):
            x = xs[layer, m]
            edge = es[layer, m - OFF if second else m]
            lt = pltpu.roll(edge, d + (48 if second else 112), 1)
            rt = pltpu.roll(edge, (16 if second else 80) - d, 1)
            xl = jnp.where(lane >= d, pltpu.roll(x, d, 1), lt)
            xr = jnp.where(lane < HC - d, pltpu.roll(x, HC - d, 1), rt)
            return jnp.concatenate([xl, x, xr], axis=0)

        def two_rows(first, second, i, carry):
            m = first + 2 * i
            b = jnp.concatenate([one_row(m, second), one_row(m + 1, second)], axis=1)
            y = jnp.dot(w, b, preferred_element_type=F32)
            ybuf[m] = y[:, :HC]
            ybuf[m + 1] = y[:, HC:]
            return carry

        def one_edge(t):
            x = es[layer, t]
            return jnp.concatenate([pltpu.roll(x, d, 1), x, pltpu.roll(x, HC - d, 1)], axis=0)

        def two_edges(i, carry):
            t = lo + 2 * i
            b = jnp.concatenate([one_edge(t), one_edge(t + 1)], axis=1)
            y = jnp.dot(w, b, preferred_element_type=F32)
            ye[t] = y[:, :HC]
            ye[t + 1] = y[:, HC:]
            return carry

        count = (SPLIT - lo) // 2
        lax.fori_loop(0, count, functools.partial(two_rows, lo, False), 0, unroll=count)
        lax.fori_loop(0, count, functools.partial(two_rows, SPLIT, True), 0, unroll=count)
        if layer < LAYERS - 1:
            lax.fori_loop(0, (TILES - 2 * lo) // 2, two_edges, 0, unroll=(TILES - 2 * lo) // 2)
        new = lo + HALO

        def total(buf, m):
            return buf[m - d, 0:64, :] + buf[m, 64:128, :] + buf[m + d, 128:192, :]

        def finish(m, carry):
            v = xs[layer, m].astype(F32) + jax.nn.gelu(total(ybuf, m))
            if layer < LAYERS - 1:
                v = v * jnp.where(m < REACH, up_ok, jnp.where(m >= REACH + HR, down_ok, 1.0))
                xs[layer + 1, m] = v.astype(BF)
            else:
                fbuf[pl.ds(pl.multiple_of((m - REACH) * CHANNELS, CHANNELS), CHANNELS), :] = v
            return carry

        def finish_edge(t, carry):
            v = (es[layer, t].astype(F32) + jax.nn.gelu(total(ye, t))) * edge_mask(t)
            es[layer + 1, t] = v.astype(BF)
            return carry

        lax.fori_loop(new, ROWS - new, finish, 0, unroll=8)
        if layer < LAYERS - 1:
            lax.fori_loop(new, TILES - new, finish_edge, 0, unroll=4)

    for c in range(CHANNELS):
        out[c] = fbuf[pl.ds(c, HR, stride=CHANNELS), :].astype(BF)
    pltpu.make_async_copy(arrived, arrived, ssem.at[0]).wait()


def kernel(pick, feed_s, rates, feed_v, win_v, gates_hbm, w_hbm, proj, taps, out,
           s0, s1, m0, m1, rows, gates, wbuf, share, grid, hot2, t1, t2, projq, wall,
           xs, es, strips, halo, ybuf, ye, fbuf, asem, arem, ssem, rsem, lsem):
    n, e, up, down, left, right = places()
    load_g = pltpu.make_async_copy(gates_hbm, gates, lsem.at[0])
    load_g.start()
    load_w = pltpu.make_async_copy(w_hbm, wbuf, lsem.at[1])
    load_w.start()
    bar = pltpu.get_barrier_semaphore()
    for i in range(1, NE):
        pl.semaphore_signal(bar, inc=1, device_id=(n, lax.rem(e + i, NE)), device_id_type=MESH)
    for i in range(1, NN):
        pl.semaphore_signal(bar, inc=1, device_id=(lax.rem(n + i, NN), e), device_id_type=MESH)
    for tn in (up, down):
        for te in (left, right):
            pl.semaphore_signal(bar, inc=1, device_id=(tn, te), device_id_type=MESH)
    load_g.wait()
    sent = exchange(pick, gates, s0, s1, m0, m1, rows, asem, arem, bar,
                    lambda: tables(win_v, feed_v, proj, taps, hot2, t1, t2, projq, wall))

    def put(i, v):
        xs[0, i + REACH] = v

    blend(feed_s, rows, wbuf, share, grid, hot2, t1, t2, projq, load_w.wait, put)
    conv(rates, wall, out, xs, es, strips, halo, ybuf, ye, fbuf, ssem, rsem)
    sent()


def per_device(gates, mixing_weight_blocks, send_pick, feed, window, proj_weight, conv_weight, rates):
    vm, sm = pl.BlockSpec(memory_space=pltpu.VMEM), pl.BlockSpec(memory_space=pltpu.SMEM)
    hbm = pl.BlockSpec(memory_space=pl.ANY)
    blk = (FEATS, GATES)
    return pl.pallas_call(
        kernel,
        out_shape=jax.ShapeDtypeStruct((CHANNELS, HR, HC), BF),
        in_specs=[sm, sm, sm, vm, vm, hbm, hbm, vm, vm],
        out_specs=vm,
        scratch_shapes=[
            pltpu.VMEM((NE, NN) + blk, BF), pltpu.VMEM((NN, NE) + blk, BF),
            pltpu.VMEM((NE, NN) + blk, BF), pltpu.VMEM((NN, NE) + blk, BF),
            pltpu.VMEM((2, ND) + blk, BF), pltpu.VMEM((PMAX,) + blk, BF),
            pltpu.VMEM((PMAX, GATES, 128), BF),
            pltpu.VMEM((PMAX * FEATS, 128), F32),
            pltpu.VMEM((128 * FEATS, 128), F32),
            pltpu.VMEM((128, 512), BF), pltpu.VMEM((512, 512), BF), pltpu.VMEM((512, 512), BF),
            pltpu.VMEM((CHANNELS, 64), BF), pltpu.VMEM((LAYERS, 3 * CHANNELS, 3 * CHANNELS), BF),
            pltpu.VMEM((LAYERS, ROWS, CHANNELS, HC), BF),
            pltpu.VMEM((LAYERS, TILES, CHANNELS, HC), BF),
            pltpu.VMEM((2, HR // 8, CHANNELS, HC), BF),
            pltpu.VMEM((2, 8, CHANNELS, HC), BF),
            pltpu.VMEM((ROWS, 3 * CHANNELS, HC), F32),
            pltpu.VMEM((TILES, 3 * CHANNELS, HC), F32),
            pltpu.VMEM((HR * CHANNELS, HC), F32),
            pltpu.SemaphoreType.DMA((4,)), pltpu.SemaphoreType.DMA((4,)),
            pltpu.SemaphoreType.DMA((1,)), pltpu.SemaphoreType.DMA((1,)),
            pltpu.SemaphoreType.DMA((2,)),
        ],
        compiler_params=pltpu.CompilerParams(
            collective_id=0, has_side_effects=True, vmem_limit_bytes=58 << 20),
        name="radar",
    )(send_pick.transpose(0, 2, 1), feed, rates, feed, window, gates, mixing_weight_blocks, proj_weight, conv_weight)


def solution(mesh):
    in_specs = (
        P(("north", "east"), None, None),
        P(("north", "east"), None, None),
        P(("north", "east"), None, None),
        P(("north", "east"), None),
        P(("north", "east"), None),
        P(),
        P(),
        P(),
    )
    return jax.shard_map(
        per_device, mesh=mesh, in_specs=in_specs, out_specs=P(None, "north", "east"), check_vma=False
    )
```

```python
import functools

import jax
import jax.numpy as jnp
from jax import lax
from jax.experimental import pallas as pl
from jax.experimental.pallas import tpu as pltpu
from jax.sharding import PartitionSpec as P

MESH = pl.DeviceIdType.MESH
NN, NE = 8, 16
ND = NN * NE
GATES = 128
FEATS = 16
CHANNELS = 64
LAYERS = 3
HALO = 4
HR, HC = 32, 128
PMAX = 256
BF, F32 = jnp.bfloat16, jnp.float32


NCH = 8
CH = PMAX // NCH
REACH = LAYERS * HALO
ROWS = HR + 2 * REACH
TILES, OFF, SPLIT = 36, 20, 28


def iota(shape, dim):
    return lax.broadcasted_iota(jnp.int32, shape, dim)


def places():
    n, e = lax.axis_index("north"), lax.axis_index("east")
    up, down = lax.rem(n + NN - 1, NN), lax.rem(n + 1, NN)
    left, right = lax.rem(e + NE - 1, NE), lax.rem(e + 1, NE)
    return n, e, up, down, left, right


def exchange(pick, gates, s0, s1, m0, m1, rows, ssem, rsem, bar, meanwhile, arrived):
    n, e, up, down, left, right = places()
    f0, f1 = rows.at[0], rows.at[1]

    def gather(t, carry):
        i, j = t // NE, lax.rem(t, NE)
        at = lax.rem(n + i, NN) * NE + lax.rem(e + j, NE)
        for k in range(2):
            p = pick[0, k, at]
            v = gates[jnp.maximum(p, 0)]
            v = jnp.where(p >= 0, v, jnp.zeros_like(v))
            if k == 0:
                s0[j, i] = v
            else:
                s1[i, j] = v
        return carry

    lax.fori_loop(0, ND, gather, 0, unroll=16)
    pl.semaphore_wait(bar, NE + NN - 2 + 4)

    def remote(src, dst, k, i, j):
        pltpu.make_async_remote_copy(
            src_ref=src, dst_ref=dst, send_sem=ssem.at[k], recv_sem=rsem.at[k],
            device_id=(lax.rem(n + i, NN), lax.rem(e + j, NE)), device_id_type=MESH,
        ).start()

    for c in range(2):
        for j in range(max(1, 8 * c), 8 * c + 8):
            remote(s0.at[j], m0.at[j], c, 0, j)
            i = j // 2
            if j % 2 == 0 and i > 0:
                remote(s1.at[i], m1.at[i], 2 + c, i, 0)
    m0[0] = s0[0]
    m1[0] = s1[0]
    meanwhile()

    def wait(count, sem):
        r = rows.at[0, pl.ds(0, count)]
        pltpu.make_async_copy(r, r, sem).wait()

    a_counts = (7 * NN, 8 * NN, 3 * NE, 4 * NE)
    b_counts = (7 * 8, 7 * 8, 15 * 4, 15 * 4)
    for c in range(2):
        wait(a_counts[2 + c], rsem.at[2 + c])
        for j in range(1, NE):
            remote(m1.at[pl.ds(4 * c, 4), j], f1.at[pl.ds(j * NN + 4 * c, 4)], 6 + c, 0, j)
        f1[pl.ds(4 * c, 4)] = m1[pl.ds(4 * c, 4), 0]
        wait(a_counts[c], rsem.at[c])
        for i in range(1, NN):
            remote(m0.at[pl.ds(8 * c, 8), i], f0.at[pl.ds(i * NE + 8 * c, 8)], 4 + c, i, 0)
        f0[pl.ds(8 * c, 8)] = m0[pl.ds(8 * c, 8), 0]
    for c in range(2):
        for k in (1, 0):
            wait(b_counts[2 * k + c], rsem.at[4 + 2 * k + c])
            arrived(k, c)

    def sent():
        for k, count in enumerate(a_counts + b_counts):
            wait(count, ssem.at[k])

    return sent


def tables(win_v, feed_v, proj, taps, hot2, t1, t2, projq, wall, entry):
    n, e, *_ = places()
    feed = feed_v[...]
    s, k = feed // 2, feed % 2
    i, j = (n + NN - s // NE) % NN, (e + NE - s % NE) % NE
    q = jnp.where(feed < 0, -1, jnp.where(k == 0, i * NE + j, ND + j * NN + i))
    down_q = jnp.transpose(jnp.broadcast_to(q, (128, PMAX)))
    number = iota((PMAX, 128), 0)
    uses = []
    for h in range(2):
        same = down_q == iota((PMAX, 128), 1) + 128 * h
        entry[:, h * 128:(h + 1) * 128] = jnp.max(jnp.where(same, number, 0), axis=0, keepdims=True)
        uses.append(jnp.where(same, 1.0, 0.0).astype(BF))
    hot = jnp.where(win_v[...] == iota((GATES, PMAX), 0), 1.0, 0.0).astype(BF)
    hot = jnp.dot(hot, jnp.concatenate(uses, axis=1), preferred_element_type=F32).astype(BF)
    hot2[...] = jnp.concatenate([hot, hot], axis=1)
    col = iota((1, 512), 1)
    i1, w1, a1, b1, j1 = col // 128, col // 32 % 4, col // 16 % 2, col // 8 % 2, col % 8
    src1 = w1 * 128 + i1 * 32 + a1 * 16 + j1 * 2 + b1
    t1[...] = jnp.where(iota((512, 512), 0) == src1, 1.0, 0.0).astype(BF)
    q2, wh2, wl2, j2 = col // 128, col // 32 % 4, col // 8 % 4, col % 8
    src2 = wh2 * 128 + wl2 * 32 + q2 * 8 + j2
    t2[...] = jnp.where(iota((512, 512), 0) == src2, 1.0, 0.0).astype(BF)
    c = iota((1, 64), 1)
    p = jnp.where(iota((64, 64), 0) == c % 16 * 4 + c // 16, 1.0, 0.0).astype(BF)
    projq[...] = jnp.dot(proj[...], p, preferred_element_type=F32).astype(BF)
    for layer in range(LAYERS):
        for a in range(3):
            line = [taps[layer, a * 3 + b].astype(F32) for b in range(3)]
            wall[layer, a * CHANNELS:(a + 1) * CHANNELS, :] = jnp.concatenate(line, axis=1).astype(BF)


def products(k, c, entry, rows, wbuf, share):
    def product(t, carry):
        q = t // 8 * NE + 8 * c + lax.rem(t, 8) if k == 0 else t // 4 * NN + 4 * c + lax.rem(t, 4)
        at = pl.multiple_of((k * ND + q) * FEATS, FEATS)
        share[pl.ds(at, FEATS), :] = jnp.dot(
            rows[k, q], wbuf[entry[0, k * ND + q]], preferred_element_type=F32)
        return carry

    lax.fori_loop(0, 64, product, 0, unroll=64)


def blend(share, grid, hot2, t1, t2, projq, put):
    for f in range(0, FEATS, 2):
        parts = []
        for g in (f, f + 1):
            v = share[pl.ds(g, PMAX, stride=FEATS), :]
            hi = v.astype(BF)
            lo = (v - hi.astype(F32)).astype(BF)
            parts.append(jnp.concatenate([hi, lo], axis=0))
        r = jnp.dot(hot2[...], jnp.concatenate(parts, axis=1), preferred_element_type=F32)
        grid[pl.ds(f, 128, stride=FEATS), :] = r[:, :128]
        grid[pl.ds(f + 1, 128, stride=FEATS), :] = r[:, 128:]

    tiles = []
    for wh in range(4):
        line = []
        for wl in range(4):
            wc = wh * 4 + wl
            blocks = [grid[pl.ds((wr * 16 + wc) * FEATS, FEATS), :] for wr in range(8)]
            line.append(jnp.concatenate(blocks, axis=0).astype(BF))
        tiles.append(jnp.concatenate(line, axis=1))
    y = jnp.dot(jnp.concatenate(tiles, axis=0), t1[...], preferred_element_type=F32).astype(BF)
    tiles = [
        jnp.concatenate([y[wh * 128:(wh + 1) * 128, i * 128:(i + 1) * 128] for wh in range(4)], axis=1)
        for i in range(4)
    ]
    z = jnp.dot(jnp.concatenate(tiles, axis=0), t2[...], preferred_element_type=F32).astype(BF)
    for wr in range(8):
        cells = []
        for i in range(4):
            r0 = (i * 8 + wr) * FEATS
            cells.append(jnp.concatenate(
                [z[r0:r0 + FEATS, q * 128:(q + 1) * 128] for q in range(4)], axis=0))
        o = jnp.dot(projq[...], jnp.concatenate(cells, axis=1), preferred_element_type=F32)
        o = jax.nn.gelu(o).astype(BF)
        for i in range(4):
            put(wr * 4 + i, o[:, i * 128:(i + 1) * 128])


def conv(rates, wall, out, xs, es, strips, halo, ybuf, ye, fbuf, ssem, rsem):
    n, e, up, down, left, right = places()
    lane = iota((CHANNELS, HC), 1)
    row_lane = iota((1, HC), 1)
    zero = jnp.zeros((CHANNELS, HC), BF)

    def remote(src, dst, dev):
        pltpu.make_async_remote_copy(
            src_ref=src, dst_ref=dst, send_sem=ssem.at[0], recv_sem=rsem.at[0],
            device_id=dev, device_id_type=MESH).start()

    for g in range(HR // 8):
        sl, sr = zero, zero
        for k in range(8):
            v = xs[0, REACH + 8 * g + k]
            here = lane // 16 == k
            sl = jnp.where(here, pltpu.roll(v, 16 * k, 1) if k else v, sl)
            sr = jnp.where(here, pltpu.roll(v, (16 * k + 16) % HC, 1) if k < 7 else v, sr)
        strips[0, g] = sl
        strips[1, g] = sr
    for side, te in ((0, right), (1, left)):
        own = strips.at[1 - side]
        remote(own, halo.at[side, pl.ds(2, 4)], (n, te))
        remote(own.at[pl.ds(2, 2)], halo.at[side, pl.ds(0, 2)], (down, te))
        remote(own.at[pl.ds(0, 2)], halo.at[side, pl.ds(6, 2)], (up, te))
    remote(xs.at[0, pl.ds(REACH, REACH)], xs.at[0, pl.ds(REACH + HR, REACH)], (up, e))
    remote(xs.at[0, pl.ds(HR, REACH)], xs.at[0, pl.ds(0, REACH)], (down, e))
    arrived = xs.at[0, pl.ds(0, 2 * REACH + 16)]
    pltpu.make_async_copy(arrived, arrived, rsem.at[0]).wait()

    @pl.when(n == 0)
    def _():
        xs[0, pl.ds(0, REACH)] = jnp.zeros((REACH, CHANNELS, HC), BF)

    @pl.when(n == NN - 1)
    def _():
        xs[0, pl.ds(REACH + HR, REACH)] = jnp.zeros((REACH, CHANNELS, HC), BF)

    up_ok, down_ok = jnp.where(n > 0, 1.0, 0.0), jnp.where(n < NN - 1, 1.0, 0.0)
    left_ok, right_ok = jnp.where(e > 0, 1.0, 0.0), jnp.where(e < NE - 1, 1.0, 0.0)
    part = row_lane % 64
    cols = jnp.where(part < 16, left_ok, jnp.where(part >= 48, right_ok, 1.0))

    def edge_mask(t):
        first = jnp.where(t < REACH, up_ok, 1.0)
        second = jnp.where(t + OFF >= REACH + HR, down_ok, 1.0)
        return cols * jnp.where(row_lane < 64, first, second)

    def assemble(t, carry):
        h0, o0 = (t + 4) // 8, lax.rem(t + 4, 8)
        h1, o1 = (t + OFF + 4) // 8, lax.rem(t + OFF + 4, 8)
        a, b = xs[0, t], xs[0, t + OFF]
        pieces = [
            pltpu.roll(halo[0, h0], lax.rem(HC - 16 * o0, HC), 1), pltpu.roll(a, 16, 1),
            pltpu.roll(a, 48, 1), pltpu.roll(halo[1, h0], lax.rem(HC + 48 - 16 * o0, HC), 1),
            pltpu.roll(halo[0, h1], lax.rem(HC + 64 - 16 * o1, HC), 1), pltpu.roll(b, 80, 1),
            pltpu.roll(b, 112, 1), pltpu.roll(halo[1, h1], lax.rem(HC + 112 - 16 * o1, HC), 1),
        ]
        v = pieces[0]
        for k in range(1, 8):
            v = jnp.where(lane // 16 == k, pieces[k], v)
        es[0, t] = (v.astype(F32) * edge_mask(t)).astype(BF)
        return carry

    lax.fori_loop(0, TILES, assemble, 0, unroll=12)

    for layer in range(LAYERS):
        d = rates[layer]
        w = wall[layer]
        lo = HALO * layer

        def one_row(m, second):
            x = xs[layer, m]
            edge = es[layer, m - OFF if second else m]
            lt = pltpu.roll(edge, d + (48 if second else 112), 1)
            rt = pltpu.roll(edge, (16 if second else 80) - d, 1)
            xl = jnp.where(lane >= d, pltpu.roll(x, d, 1), lt)
            xr = jnp.where(lane < HC - d, pltpu.roll(x, HC - d, 1), rt)
            return jnp.concatenate([xl, x, xr], axis=0)

        def two_rows(first, second, i, carry):
            m = first + 2 * i
            b = jnp.concatenate([one_row(m, second), one_row(m + 1, second)], axis=1)
            y = jnp.dot(w, b, preferred_element_type=F32)
            ybuf[m] = y[:, :HC]
            ybuf[m + 1] = y[:, HC:]
            return carry

        def one_edge(t):
            x = es[layer, t]
            return jnp.concatenate([pltpu.roll(x, d, 1), x, pltpu.roll(x, HC - d, 1)], axis=0)

        def two_edges(i, carry):
            t = lo + 2 * i
            b = jnp.concatenate([one_edge(t), one_edge(t + 1)], axis=1)
            y = jnp.dot(w, b, preferred_element_type=F32)
            ye[t] = y[:, :HC]
            ye[t + 1] = y[:, HC:]
            return carry

        count = (SPLIT - lo) // 2
        lax.fori_loop(0, count, functools.partial(two_rows, lo, False), 0, unroll=count)
        lax.fori_loop(0, count, functools.partial(two_rows, SPLIT, True), 0, unroll=count)
        if layer < LAYERS - 1:
            lax.fori_loop(0, (TILES - 2 * lo) // 2, two_edges, 0, unroll=(TILES - 2 * lo) // 2)
        new = lo + HALO

        def total(buf, m):
            return buf[m - d, 0:64, :] + buf[m, 64:128, :] + buf[m + d, 128:192, :]

        def finish(m, carry):
            v = xs[layer, m].astype(F32) + jax.nn.gelu(total(ybuf, m))
            if layer < LAYERS - 1:
                v = v * jnp.where(m < REACH, up_ok, jnp.where(m >= REACH + HR, down_ok, 1.0))
                xs[layer + 1, m] = v.astype(BF)
            else:
                fbuf[pl.ds(pl.multiple_of((m - REACH) * CHANNELS, CHANNELS), CHANNELS), :] = v
            return carry

        def finish_edge(t, carry):
            v = (es[layer, t].astype(F32) + jax.nn.gelu(total(ye, t))) * edge_mask(t)
            es[layer + 1, t] = v.astype(BF)
            return carry

        lax.fori_loop(new, ROWS - new, finish, 0, unroll=8)
        if layer < LAYERS - 1:
            lax.fori_loop(new, TILES - new, finish_edge, 0, unroll=4)

    for c in range(CHANNELS):
        out[c] = fbuf[pl.ds(c, HR, stride=CHANNELS), :].astype(BF)
    pltpu.make_async_copy(arrived, arrived, ssem.at[0]).wait()


def kernel(pick_h, feed_h, rates_h, win_h, gates_h, w_h, proj_h, taps_h, out,
           s0, s1, m0, m1, rows, gates, wbuf, share, grid, hot2, t1, t2, projq, wall,
           xs, es, strips, halo, ybuf, ye, fbuf, pick, entry, entry_v, rates, feed_v, win_v, proj, taps,
           asem, arem, ssem, rsem, lsem):
    n, e, up, down, left, right = places()
    pairs = [(pick_h, pick), (gates_h, gates), (rates_h, rates), (feed_h, feed_v), (win_h, win_v), (proj_h, proj), (taps_h, taps), (w_h, wbuf)]
    loads = [pltpu.make_async_copy(src, dst, lsem.at[k]) for k, (src, dst) in enumerate(pairs)]
    for load in loads:
        load.start()
    bar = pltpu.get_barrier_semaphore()
    for i in range(1, NE):
        pl.semaphore_signal(bar, inc=1, device_id=(n, lax.rem(e + i, NE)), device_id_type=MESH)
    for i in range(1, NN):
        pl.semaphore_signal(bar, inc=1, device_id=(lax.rem(n + i, NN), e), device_id_type=MESH)
    for tn in (up, down):
        for te in (left, right):
            pl.semaphore_signal(bar, inc=1, device_id=(tn, te), device_id_type=MESH)
    loads[0].wait()
    loads[1].wait()

    def meanwhile():
        for load in loads[2:7]:
            load.wait()
        tables(win_v, feed_v, proj, taps, hot2, t1, t2, projq, wall, entry_v)
        to_scalar = pltpu.make_async_copy(entry_v, entry, lsem.at[8])
        to_scalar.start()
        to_scalar.wait()
        loads[7].wait()

    sent = exchange(pick, gates, s0, s1, m0, m1, rows, asem, arem, bar, meanwhile,
                    lambda k, c: products(k, c, entry, rows, wbuf, share))

    def put(i, v):
        xs[0, i + REACH] = v

    blend(share, grid, hot2, t1, t2, projq, put)
    conv(rates, wall, out, xs, es, strips, halo, ybuf, ye, fbuf, ssem, rsem)
    sent()


def per_device(gates, mixing_weight_blocks, send_pick, feed, window, proj_weight, conv_weight, rates):
    hbm = pl.BlockSpec(memory_space=pltpu.HBM)
    blk = (FEATS, GATES)
    return pl.pallas_call(
        kernel,
        out_shape=jax.ShapeDtypeStruct((CHANNELS, HR, HC), BF),
        in_specs=[hbm] * 8,
        out_specs=pl.BlockSpec(memory_space=pltpu.VMEM),
        scratch_shapes=[
            pltpu.VMEM((NE, NN) + blk, BF), pltpu.VMEM((NN, NE) + blk, BF),
            pltpu.VMEM((NE, NN) + blk, BF), pltpu.VMEM((NN, NE) + blk, BF),
            pltpu.VMEM((2, ND) + blk, BF), pltpu.VMEM((PMAX,) + blk, BF),
            pltpu.VMEM((PMAX, GATES, 128), BF),
            pltpu.VMEM((PMAX * FEATS, 128), F32),
            pltpu.VMEM((128 * FEATS, 128), F32),
            pltpu.VMEM((128, 512), BF), pltpu.VMEM((512, 512), BF), pltpu.VMEM((512, 512), BF),
            pltpu.VMEM((CHANNELS, 64), BF), pltpu.VMEM((LAYERS, 3 * CHANNELS, 3 * CHANNELS), BF),
            pltpu.VMEM((LAYERS, ROWS, CHANNELS, HC), BF),
            pltpu.VMEM((LAYERS, TILES, CHANNELS, HC), BF),
            pltpu.VMEM((2, HR // 8, CHANNELS, HC), BF),
            pltpu.VMEM((2, 8, CHANNELS, HC), BF),
            pltpu.VMEM((ROWS, 3 * CHANNELS, HC), F32),
            pltpu.VMEM((TILES, 3 * CHANNELS, HC), F32),
            pltpu.VMEM((HR * CHANNELS, HC), F32),
            pltpu.SMEM((1, 2, ND), jnp.int32), pltpu.SMEM((1, PMAX), jnp.int32), pltpu.VMEM((1, PMAX), jnp.int32),
            pltpu.SMEM((LAYERS,), jnp.int32), pltpu.VMEM((1, PMAX), jnp.int32), pltpu.VMEM((1, PMAX), jnp.int32),
            pltpu.VMEM((CHANNELS, 64), BF), pltpu.VMEM((LAYERS, 9, CHANNELS, CHANNELS), BF),
            pltpu.SemaphoreType.DMA((8,)), pltpu.SemaphoreType.DMA((8,)),
            pltpu.SemaphoreType.DMA((1,)), pltpu.SemaphoreType.DMA((1,)),
            pltpu.SemaphoreType.DMA((9,)),
        ],
        compiler_params=pltpu.CompilerParams(
            collective_id=0, has_side_effects=True, vmem_limit_bytes=58 << 20),
        name="radar",
    )(send_pick.transpose(0, 2, 1), feed, rates, window, gates, mixing_weight_blocks, proj_weight, conv_weight)


def solution(mesh):
    in_specs = (
        P(("north", "east"), None, None),
        P(("north", "east"), None, None),
        P(("north", "east"), None, None),
        P(("north", "east"), None),
        P(("north", "east"), None),
        P(),
        P(),
        P(),
    )
    return jax.shard_map(
        per_device, mesh=mesh, in_specs=in_specs, out_specs=P(None, "north", "east"), check_vma=False
    )
```

```python
import functools

import jax
import jax.numpy as jnp
from jax import lax
from jax.experimental import pallas as pl
from jax.experimental.pallas import tpu as pltpu
from jax.sharding import PartitionSpec as P

MESH = pl.DeviceIdType.MESH
NN, NE = 8, 16
ND = NN * NE
GATES = 128
FEATS = 16
CHANNELS = 64
LAYERS = 3
HALO = 4
HR, HC = 32, 128
PMAX = 256
BF, F32 = jnp.bfloat16, jnp.float32


NCH = 8
CH = PMAX // NCH
REACH = LAYERS * HALO
ROWS = HR + 2 * REACH
TILES, OFF, SPLIT = 36, 20, 28


def iota(shape, dim):
    return lax.broadcasted_iota(jnp.int32, shape, dim)


def places():
    n, e = lax.axis_index("north"), lax.axis_index("east")
    up, down = lax.rem(n + NN - 1, NN), lax.rem(n + 1, NN)
    left, right = lax.rem(e + NE - 1, NE), lax.rem(e + 1, NE)
    return n, e, up, down, left, right


def exchange(pick, gates, s0, s1, m0, m1, rows, ssem, rsem, bar, meanwhile, arrived):
    n, e, up, down, left, right = places()
    f0, f1 = rows.at[0], rows.at[1]

    def gather(t, carry):
        i, j = t // NE, lax.rem(t, NE)
        at = lax.rem(n + i, NN) * NE + lax.rem(e + j, NE)
        for k in range(2):
            p = pick[0, k, at]
            v = gates[jnp.maximum(p, 0)]
            v = jnp.where(p >= 0, v, jnp.zeros_like(v))
            if k == 0:
                s0[j, i] = v
            else:
                s1[i, j] = v
        return carry

    lax.fori_loop(0, ND, gather, 0, unroll=16)
    pl.semaphore_wait(bar, NE + NN - 2 + 4)

    def remote(src, dst, k, i, j):
        pltpu.make_async_remote_copy(
            src_ref=src, dst_ref=dst, send_sem=ssem.at[k], recv_sem=rsem.at[k],
            device_id=(lax.rem(n + i, NN), lax.rem(e + j, NE)), device_id_type=MESH,
        ).start()

    for c in range(2):
        for j in range(max(1, 8 * c), 8 * c + 8):
            remote(s0.at[j], m0.at[j], c, 0, j)
            i = j // 2
            if j % 2 == 0 and i > 0:
                remote(s1.at[i], m1.at[i], 2 + c, i, 0)
    m0[0] = s0[0]
    m1[0] = s1[0]
    meanwhile()

    def wait(count, sem):
        r = rows.at[0, pl.ds(0, count)]
        pltpu.make_async_copy(r, r, sem).wait()

    a_counts = (7 * NN, 8 * NN, 3 * NE, 4 * NE)
    b_counts = (7 * 8, 7 * 8, 15 * 4, 15 * 4)
    for c in range(2):
        wait(a_counts[2 + c], rsem.at[2 + c])
        for j in range(1, NE):
            remote(m1.at[pl.ds(4 * c, 4), j], f1.at[pl.ds(j * NN + 4 * c, 4)], 6 + c, 0, j)
        f1[pl.ds(4 * c, 4)] = m1[pl.ds(4 * c, 4), 0]
        wait(a_counts[c], rsem.at[c])
        for i in range(1, NN):
            remote(m0.at[pl.ds(8 * c, 8), i], f0.at[pl.ds(i * NE + 8 * c, 8)], 4 + c, i, 0)
        f0[pl.ds(8 * c, 8)] = m0[pl.ds(8 * c, 8), 0]
    for c in range(2):
        for k in (1, 0):
            wait(b_counts[2 * k + c], rsem.at[4 + 2 * k + c])
            arrived(k, c)

    def sent():
        for k, count in enumerate(a_counts + b_counts):
            wait(count, ssem.at[k])

    return sent


def tables(win_v, feed_v, proj, taps, hot2, t1, t2, projq, wall, entry):
    n, e, *_ = places()
    feed = feed_v[...]
    s, k = feed // 2, feed % 2
    i, j = (n + NN - s // NE) % NN, (e + NE - s % NE) % NE
    q = jnp.where(feed < 0, -1, jnp.where(k == 0, i * NE + j, ND + j * NN + i))
    down_q = jnp.transpose(jnp.broadcast_to(q, (128, PMAX)))
    number = iota((PMAX, 128), 0)
    uses = []
    for h in range(2):
        same = down_q == iota((PMAX, 128), 1) + 128 * h
        entry[:, h * 128:(h + 1) * 128] = jnp.max(jnp.where(same, number, 0), axis=0, keepdims=True)
        uses.append(jnp.where(same, 1.0, 0.0).astype(BF))
    hot = jnp.where(win_v[...] == iota((GATES, PMAX), 0), 1.0, 0.0).astype(BF)
    hot = jnp.dot(hot, jnp.concatenate(uses, axis=1), preferred_element_type=F32).astype(BF)
    hot2[...] = jnp.concatenate([hot, hot], axis=1)
    col = iota((1, 512), 1)
    i1, w1, a1, b1, j1 = col // 128, col // 32 % 4, col // 16 % 2, col // 8 % 2, col % 8
    src1 = w1 * 128 + i1 * 32 + a1 * 16 + j1 * 2 + b1
    t1[...] = jnp.where(iota((512, 512), 0) == src1, 1.0, 0.0).astype(BF)
    q2, wh2, wl2, j2 = col // 128, col // 32 % 4, col // 8 % 4, col % 8
    src2 = wh2 * 128 + wl2 * 32 + q2 * 8 + j2
    t2[...] = jnp.where(iota((512, 512), 0) == src2, 1.0, 0.0).astype(BF)
    c = iota((1, 64), 1)
    p = jnp.where(iota((64, 64), 0) == c % 16 * 4 + c // 16, 1.0, 0.0).astype(BF)
    projq[...] = jnp.dot(proj[...], p, preferred_element_type=F32).astype(BF)
    for layer in range(LAYERS):
        for a in range(3):
            line = [taps[layer, a * 3 + b].astype(F32) for b in range(3)]
            wall[layer, a * CHANNELS:(a + 1) * CHANNELS, :] = jnp.concatenate(line, axis=1).astype(BF)


def products(k, c, entry, rows, wbuf, share):
    def product(t, carry):
        q = t // 8 * NE + 8 * c + lax.rem(t, 8) if k == 0 else t // 4 * NN + 4 * c + lax.rem(t, 4)
        at = pl.multiple_of((k * ND + q) * FEATS, FEATS)
        share[pl.ds(at, FEATS), :] = jnp.dot(
            rows[k, q], wbuf[entry[0, k * ND + q]], preferred_element_type=F32)
        return carry

    lax.fori_loop(0, 64, product, 0, unroll=64)


def blend(share, grid, hot2, t1, t2, projq, put, send):
    for f in range(0, FEATS, 2):
        parts = []
        for g in (f, f + 1):
            v = share[pl.ds(g, PMAX, stride=FEATS), :]
            hi = v.astype(BF)
            lo = (v - hi.astype(F32)).astype(BF)
            parts.append(jnp.concatenate([hi, lo], axis=0))
        r = jnp.dot(hot2[...], jnp.concatenate(parts, axis=1), preferred_element_type=F32)
        grid[pl.ds(f, 128, stride=FEATS), :] = r[:, :128]
        grid[pl.ds(f + 1, 128, stride=FEATS), :] = r[:, 128:]

    tiles = []
    for wh in range(4):
        line = []
        for wl in range(4):
            wc = wh * 4 + wl
            blocks = [grid[pl.ds((wr * 16 + wc) * FEATS, FEATS), :] for wr in range(8)]
            line.append(jnp.concatenate(blocks, axis=0).astype(BF))
        tiles.append(jnp.concatenate(line, axis=1))
    y = jnp.dot(jnp.concatenate(tiles, axis=0), t1[...], preferred_element_type=F32).astype(BF)
    tiles = [
        jnp.concatenate([y[wh * 128:(wh + 1) * 128, i * 128:(i + 1) * 128] for wh in range(4)], axis=1)
        for i in range(4)
    ]
    z = jnp.dot(jnp.concatenate(tiles, axis=0), t2[...], preferred_element_type=F32).astype(BF)
    for wr in range(8):
        cells = []
        for i in range(4):
            r0 = (i * 8 + wr) * FEATS
            cells.append(jnp.concatenate(
                [z[r0:r0 + FEATS, q * 128:(q + 1) * 128] for q in range(4)], axis=0))
        o = jnp.dot(projq[...], jnp.concatenate(cells, axis=1), preferred_element_type=F32)
        o = jax.nn.gelu(o).astype(BF)
        for i in range(4):
            put(wr * 4 + i, o[:, i * 128:(i + 1) * 128])
        if wr % 2:
            send(wr // 2)


def send_halo(g, xs, strips, halo, ssem, rsem):
    n, e, up, down, left, right = places()
    lane = iota((CHANNELS, HC), 1)

    def remote(src, dst, dev, k=0):
        pltpu.make_async_remote_copy(
            src_ref=src, dst_ref=dst, send_sem=ssem.at[k], recv_sem=rsem.at[k],
            device_id=dev, device_id_type=MESH).start()

    sl = sr = jnp.zeros((CHANNELS, HC), BF)
    for k in range(8):
        v = xs[0, REACH + 8 * g + k]
        here = lane // 16 == k
        sl = jnp.where(here, pltpu.roll(v, 16 * k, 1) if k else v, sl)
        sr = jnp.where(here, pltpu.roll(v, (16 * k + 16) % HC, 1) if k < 7 else v, sr)
    strips[0, g] = sl
    strips[1, g] = sr
    for side, te in ((0, right), (1, left)):
        own = strips.at[1 - side, g]
        remote(own, halo.at[side, g + 2], (n, te))
        if g >= 2:
            remote(own, halo.at[side, g - 2], (down, te))
        else:
            remote(own, halo.at[side, g + 6], (up, te))
    if g == 1:
        remote(xs.at[0, pl.ds(REACH, REACH)], xs.at[0, pl.ds(REACH + HR, REACH)], (up, e), 1)
    if g == 3:
        remote(xs.at[0, pl.ds(HR, REACH)], xs.at[0, pl.ds(0, REACH)], (down, e), 1)


def conv(rates, wall, out, xs, es, halo, ybuf, ye, fbuf, ssem, rsem):
    n, e, up, down, left, right = places()
    lane = iota((CHANNELS, HC), 1)
    row_lane = iota((1, HC), 1)

    up_ok, down_ok = jnp.where(n > 0, 1.0, 0.0), jnp.where(n < NN - 1, 1.0, 0.0)
    left_ok, right_ok = jnp.where(e > 0, 1.0, 0.0), jnp.where(e < NE - 1, 1.0, 0.0)
    part = row_lane % 64
    cols = jnp.where(part < 16, left_ok, jnp.where(part >= 48, right_ok, 1.0))

    def edge_mask(t):
        first = jnp.where(t < REACH, up_ok, 1.0)
        second = jnp.where(t + OFF >= REACH + HR, down_ok, 1.0)
        return cols * jnp.where(row_lane < 64, first, second)

    def assemble(t):
        h0, o0 = (t + 4) // 8, lax.rem(t + 4, 8)
        h1, o1 = (t + OFF + 4) // 8, lax.rem(t + OFF + 4, 8)
        a, b = xs[0, t], xs[0, t + OFF]
        pieces = [
            pltpu.roll(halo[0, h0], lax.rem(HC - 16 * o0, HC), 1), pltpu.roll(a, 16, 1),
            pltpu.roll(a, 48, 1), pltpu.roll(halo[1, h0], lax.rem(HC + 48 - 16 * o0, HC), 1),
            pltpu.roll(halo[0, h1], lax.rem(HC + 64 - 16 * o1, HC), 1), pltpu.roll(b, 80, 1),
            pltpu.roll(b, 112, 1), pltpu.roll(halo[1, h1], lax.rem(HC + 112 - 16 * o1, HC), 1),
        ]
        v = pieces[0]
        for k in range(1, 8):
            v = jnp.where(lane // 16 == k, pieces[k], v)
        es[0, t] = (v.astype(F32) * edge_mask(t)).astype(BF)

    def loop(lo, hi, body, unroll):
        lax.fori_loop(lo, hi, lambda m, carry: (body(m), carry)[1], 0, unroll=unroll)

    def total(buf, m, d):
        return buf[m - d, 0:64, :] + buf[m, 64:128, :] + buf[m + d, 128:192, :]

    def layer_ops(layer):
        d = rates[layer]
        w = wall[layer]
        y_of = ybuf.at[layer % 2]

        def one_row(m, second):
            x = xs[layer, m]
            if second is None:
                lt = rt = jnp.zeros((CHANNELS, HC), BF)
            else:
                edge = es[layer, m - OFF if second else m]
                lt = pltpu.roll(edge, d + (48 if second else 112), 1)
                rt = pltpu.roll(edge, (16 if second else 80) - d, 1)
            xl = jnp.where(lane >= d, pltpu.roll(x, d, 1), lt)
            xr = jnp.where(lane < HC - d, pltpu.roll(x, HC - d, 1), rt)
            return jnp.concatenate([xl, x, xr], axis=0)

        def one_edge(t):
            x = es[layer, t]
            return jnp.concatenate([pltpu.roll(x, d, 1), x, pltpu.roll(x, HC - d, 1)], axis=0)

        def pair(one, buf, m):
            y = jnp.dot(w, jnp.concatenate([one(m), one(m + 1)], axis=1), preferred_element_type=F32)
            buf[m] = y[:, :HC]
            buf[m + 1] = y[:, HC:]

        def rows(first, last, second):
            count = (last - first) // 2
            loop(0, count, lambda i: pair(lambda m: one_row(m, second), y_of, first + 2 * i), count)

        def edges(first, last):
            count = (last - first) // 2
            loop(0, count, lambda i: pair(one_edge, ye, first + 2 * i), count)

        def finish(m):
            v = xs[layer, m].astype(F32) + jax.nn.gelu(total(y_of, m, d))
            if layer < LAYERS - 1:
                v = v * jnp.where(m < REACH, up_ok, jnp.where(m >= REACH + HR, down_ok, 1.0))
                xs[layer + 1, m] = v.astype(BF)
            else:
                fbuf[pl.ds(pl.multiple_of((m - REACH) * CHANNELS, CHANNELS), CHANNELS), :] = v

        def finish_edge(t):
            v = (es[layer, t].astype(F32) + jax.nn.gelu(total(ye, t, d))) * edge_mask(t)
            es[layer + 1, t] = v.astype(BF)

        def repair(second):
            def row(m):
                edge = es[layer + 1, m - OFF if second else m]
                v = xs[layer + 1, m]
                v = jnp.where(lane < 2 * HALO, pltpu.roll(edge, 48 if second else 112, 1), v)
                v = jnp.where(lane >= HC - 2 * HALO, pltpu.roll(edge, 16 if second else 80, 1), v)
                xs[layer + 1, m] = v
            return row

        return rows, edges, finish, finish_edge, repair

    arrived = [xs.at[0, pl.ds(0, 16)], xs.at[0, pl.ds(0, 2 * REACH)]]
    top, bottom = REACH, REACH + HR
    rows0, edges0, finish0, finish_edge0, _ = layer_ops(0)
    rows1, edges1, finish1, finish_edge1, repair = layer_ops(1)
    rows0(top, bottom, None)
    loop(top + HALO, bottom - HALO, finish0, 24)
    rows1(top + HALO, bottom - HALO, None)
    loop(top + 2 * HALO, bottom - 2 * HALO, finish1, 16)
    pltpu.make_async_copy(arrived[1], arrived[1], rsem.at[1]).wait()

    @pl.when(n == 0)
    def _():
        xs[0, pl.ds(0, REACH)] = jnp.zeros((REACH, CHANNELS, HC), BF)

    @pl.when(n == NN - 1)
    def _():
        xs[0, pl.ds(REACH + HR, REACH)] = jnp.zeros((REACH, CHANNELS, HC), BF)

    rows0(0, top, None)
    rows0(bottom, ROWS, None)
    loop(HALO, top + HALO, finish0, 12)
    loop(bottom - HALO, ROWS - HALO, finish0, 12)
    rows1(HALO, top + HALO, None)
    rows1(bottom - HALO, ROWS - HALO, None)
    loop(2 * HALO, top + 2 * HALO, finish1, 12)
    loop(bottom - 2 * HALO, ROWS - 2 * HALO, finish1, 12)
    pltpu.make_async_copy(arrived[0], arrived[0], rsem.at[0]).wait()
    loop(0, TILES, assemble, 12)
    edges0(0, TILES)
    loop(HALO, TILES - HALO, finish_edge0, 14)
    edges1(HALO, TILES - HALO)
    loop(2 * HALO, TILES - 2 * HALO, finish_edge1, 10)
    loop(2 * HALO, SPLIT, repair(False), 20)
    loop(SPLIT, ROWS - 2 * HALO, repair(True), 20)
    rows2, _, finish2, _, _ = layer_ops(2)
    rows2(2 * HALO, SPLIT, False)
    rows2(SPLIT, ROWS - 2 * HALO, True)
    loop(REACH, REACH + HR, finish2, 16)

    for c in range(CHANNELS):
        out[c] = fbuf[pl.ds(c, HR, stride=CHANNELS), :].astype(BF)
    for k in range(2):
        pltpu.make_async_copy(arrived[k], arrived[k], ssem.at[k]).wait()


def kernel(pick_h, feed_h, rates_h, win_h, gates_h, w_h, proj_h, taps_h, out,
           s0, s1, m0, m1, rows, gates, wbuf, share, grid, hot2, t1, t2, projq, wall,
           xs, es, strips, halo, ybuf, ye, fbuf, pick, entry, entry_v, rates, feed_v, win_v, proj, taps,
           asem, arem, ssem, rsem, lsem):
    n, e, up, down, left, right = places()
    pairs = [(pick_h, pick), (gates_h, gates), (rates_h, rates), (feed_h, feed_v), (win_h, win_v), (proj_h, proj), (taps_h, taps), (w_h, wbuf)]
    loads = [pltpu.make_async_copy(src, dst, lsem.at[k]) for k, (src, dst) in enumerate(pairs)]
    for load in loads:
        load.start()
    bar = pltpu.get_barrier_semaphore()
    for i in range(1, NE):
        pl.semaphore_signal(bar, inc=1, device_id=(n, lax.rem(e + i, NE)), device_id_type=MESH)
    for i in range(1, NN):
        pl.semaphore_signal(bar, inc=1, device_id=(lax.rem(n + i, NN), e), device_id_type=MESH)
    for tn in (up, down):
        for te in (left, right):
            pl.semaphore_signal(bar, inc=1, device_id=(tn, te), device_id_type=MESH)
    loads[0].wait()
    loads[1].wait()

    def meanwhile():
        for load in loads[2:7]:
            load.wait()
        tables(win_v, feed_v, proj, taps, hot2, t1, t2, projq, wall, entry_v)
        to_scalar = pltpu.make_async_copy(entry_v, entry, lsem.at[8])
        to_scalar.start()
        to_scalar.wait()
        loads[7].wait()

    sent = exchange(pick, gates, s0, s1, m0, m1, rows, asem, arem, bar, meanwhile,
                    lambda k, c: products(k, c, entry, rows, wbuf, share))

    def put(i, v):
        xs[0, i + REACH] = v

    blend(share, grid, hot2, t1, t2, projq, put,
          lambda g: send_halo(g, xs, strips, halo, ssem, rsem))
    conv(rates, wall, out, xs, es, halo, ybuf, ye, fbuf, ssem, rsem)
    sent()


def per_device(gates, mixing_weight_blocks, send_pick, feed, window, proj_weight, conv_weight, rates):
    hbm = pl.BlockSpec(memory_space=pltpu.HBM)
    blk = (FEATS, GATES)
    return pl.pallas_call(
        kernel,
        out_shape=jax.ShapeDtypeStruct((CHANNELS, HR, HC), BF),
        in_specs=[hbm] * 8,
        out_specs=pl.BlockSpec(memory_space=pltpu.VMEM),
        scratch_shapes=[
            pltpu.VMEM((NE, NN) + blk, BF), pltpu.VMEM((NN, NE) + blk, BF),
            pltpu.VMEM((NE, NN) + blk, BF), pltpu.VMEM((NN, NE) + blk, BF),
            pltpu.VMEM((2, ND) + blk, BF), pltpu.VMEM((PMAX,) + blk, BF),
            pltpu.VMEM((PMAX, GATES, 128), BF),
            pltpu.VMEM((PMAX * FEATS, 128), F32),
            pltpu.VMEM((128 * FEATS, 128), F32),
            pltpu.VMEM((128, 512), BF), pltpu.VMEM((512, 512), BF), pltpu.VMEM((512, 512), BF),
            pltpu.VMEM((CHANNELS, 64), BF), pltpu.VMEM((LAYERS, 3 * CHANNELS, 3 * CHANNELS), BF),
            pltpu.VMEM((LAYERS, ROWS, CHANNELS, HC), BF),
            pltpu.VMEM((LAYERS, TILES, CHANNELS, HC), BF),
            pltpu.VMEM((2, HR // 8, CHANNELS, HC), BF),
            pltpu.VMEM((2, 8, CHANNELS, HC), BF),
            pltpu.VMEM((2, ROWS, 3 * CHANNELS, HC), F32),
            pltpu.VMEM((TILES, 3 * CHANNELS, HC), F32),
            pltpu.VMEM((HR * CHANNELS, HC), F32),
            pltpu.SMEM((1, 2, ND), jnp.int32), pltpu.SMEM((1, PMAX), jnp.int32), pltpu.VMEM((1, PMAX), jnp.int32),
            pltpu.SMEM((LAYERS,), jnp.int32), pltpu.VMEM((1, PMAX), jnp.int32), pltpu.VMEM((1, PMAX), jnp.int32),
            pltpu.VMEM((CHANNELS, 64), BF), pltpu.VMEM((LAYERS, 9, CHANNELS, CHANNELS), BF),
            pltpu.SemaphoreType.DMA((8,)), pltpu.SemaphoreType.DMA((8,)),
            pltpu.SemaphoreType.DMA((2,)), pltpu.SemaphoreType.DMA((2,)),
            pltpu.SemaphoreType.DMA((9,)),
        ],
        compiler_params=pltpu.CompilerParams(
            collective_id=0, has_side_effects=True, vmem_limit_bytes=58 << 20),
        name="radar",
    )(send_pick.transpose(0, 2, 1), feed, rates, window, gates, mixing_weight_blocks, proj_weight, conv_weight)


def solution(mesh):
    in_specs = (
        P(("north", "east"), None, None),
        P(("north", "east"), None, None),
        P(("north", "east"), None, None),
        P(("north", "east"), None),
        P(("north", "east"), None),
        P(),
        P(),
        P(),
    )
    return jax.shard_map(
        per_device, mesh=mesh, in_specs=in_specs, out_specs=P(None, "north", "east"), check_vma=False
    )
```

```python
import functools

import jax
import jax.numpy as jnp
from jax import lax
from jax.experimental import pallas as pl
from jax.experimental.pallas import tpu as pltpu
from jax.sharding import PartitionSpec as P

MESH = pl.DeviceIdType.MESH
NN, NE = 8, 16
ND = NN * NE
GATES = 128
FEATS = 16
CHANNELS = 64
LAYERS = 3
HALO = 4
HR, HC = 32, 128
PMAX = 256
BF, F32 = jnp.bfloat16, jnp.float32


CHUNKS = 4
CI, CJ = NN // CHUNKS, NE // CHUNKS
GROUP = CI * NE
REACH = LAYERS * HALO
ROWS = HR + 2 * REACH
TILES, OFF, SPLIT = 36, 20, 28


def iota(shape, dim):
    return lax.broadcasted_iota(jnp.int32, shape, dim)


def places():
    n, e = lax.axis_index("north"), lax.axis_index("east")
    up, down = lax.rem(n + NN - 1, NN), lax.rem(n + 1, NN)
    left, right = lax.rem(e + NE - 1, NE), lax.rem(e + 1, NE)
    return n, e, up, down, left, right


def exchange(pick, gates, s0, s1, m0, m1, rows, ssem, rsem, bar, gathered, meanwhile, arrived):
    n, e, up, down, left, right = places()
    f0, f1 = rows.at[0], rows.at[1]

    def gather(t, carry):
        i, j = t // NE, lax.rem(t, NE)
        at = lax.rem(n + i, NN) * NE + lax.rem(e + j, NE)
        for k in range(2):
            p = pick[0, k, at]
            v = gates[jnp.maximum(p, 0)]
            v = jnp.where(p >= 0, v, jnp.zeros_like(v))
            if k == 0:
                s0[j, i] = v
            else:
                s1[i, j] = v
        return carry

    lax.fori_loop(0, ND, gather, 0, unroll=64)
    gathered()
    pl.semaphore_wait(bar, NE + NN - 2 + 4)

    def remote(src, dst, k, i, j):
        pltpu.make_async_remote_copy(
            src_ref=src, dst_ref=dst, send_sem=ssem.at[k], recv_sem=rsem.at[k],
            device_id=(lax.rem(n + i, NN), lax.rem(e + j, NE)), device_id_type=MESH,
        ).start()

    for c in range(CHUNKS):
        for j in range(max(1, CJ * c), CJ * c + CJ):
            remote(s0.at[j], m0.at[j], c, 0, j)
            i = j // 2
            if j % 2 == 0 and i > 0:
                remote(s1.at[i], m1.at[i], CHUNKS + c, i, 0)
    m0[0] = s0[0]
    m1[0] = s1[0]
    meanwhile()

    def wait(count, sem):
        r = rows.at[0, pl.ds(0, count)]
        pltpu.make_async_copy(r, r, sem).wait()

    a_counts = [(CJ - (c == 0)) * NN for c in range(CHUNKS)] + [(CI - (c == 0)) * NE for c in range(CHUNKS)]
    b_counts = [(NN - 1) * CJ] * CHUNKS + [(NE - 1) * CI] * CHUNKS
    counts = a_counts + b_counts
    for c in range(CHUNKS):
        wait(counts[CHUNKS + c], rsem.at[CHUNKS + c])
        for j in range(1, NE):
            remote(m1.at[pl.ds(CI * c, CI), j], f1.at[pl.ds(j * NN + CI * c, CI)], 3 * CHUNKS + c, 0, j)
        f1[pl.ds(CI * c, CI)] = m1[pl.ds(CI * c, CI), 0]
        wait(counts[c], rsem.at[c])
        for i in range(1, NN):
            remote(m0.at[pl.ds(CJ * c, CJ), i], f0.at[pl.ds(i * NE + CJ * c, CJ)], 2 * CHUNKS + c, i, 0)
        f0[pl.ds(CJ * c, CJ)] = m0[pl.ds(CJ * c, CJ), 0]
    for c in range(CHUNKS):
        for k in (1, 0):
            at = (2 + k) * CHUNKS + c
            wait(counts[at], rsem.at[at])
            arrived(k, c)

    def sent():
        for k, count in enumerate(counts):
            wait(count, ssem.at[k])

    return sent


def tables(win_v, feed_v, proj, taps, hot2, t1, t2, projq, wall, entry):
    n, e, *_ = places()
    feed = feed_v[...]
    s, k = feed // 2, feed % 2
    i, j = (n + NN - s // NE) % NN, (e + NE - s % NE) % NE
    q0 = j // CJ * 2 * GROUP + i * CJ + j % CJ
    q1 = i // CI * 2 * GROUP + GROUP + j * CI + i % CI
    q = jnp.where(feed < 0, -1, jnp.where(k == 0, q0, q1))
    down_q = jnp.transpose(jnp.broadcast_to(q, (128, PMAX)))
    number = iota((PMAX, 128), 0)
    uses = []
    for h in range(2):
        same = down_q == iota((PMAX, 128), 1) + 128 * h
        entry[:, h * 128:(h + 1) * 128] = jnp.max(jnp.where(same, number, 0), axis=0, keepdims=True)
        uses.append(jnp.where(same, 1.0, 0.0).astype(BF))
    hot = jnp.where(win_v[...] == iota((GATES, PMAX), 0), 1.0, 0.0).astype(BF)
    hot = jnp.dot(hot, jnp.concatenate(uses, axis=1), preferred_element_type=F32).astype(BF)
    hot2[...] = jnp.concatenate([hot[:, :128], hot[:, :128], hot[:, 128:], hot[:, 128:]], axis=1)
    col = iota((1, 512), 1)
    i1, w1, a1, b1, j1 = col // 128, col // 32 % 4, col // 16 % 2, col // 8 % 2, col % 8
    src1 = w1 * 128 + i1 * 32 + a1 * 16 + j1 * 2 + b1
    t1[...] = jnp.where(iota((512, 512), 0) == src1, 1.0, 0.0).astype(BF)
    q2, wh2, wl2, j2 = col // 128, col // 32 % 4, col // 8 % 4, col % 8
    src2 = wh2 * 128 + wl2 * 32 + q2 * 8 + j2
    t2[...] = jnp.where(iota((512, 512), 0) == src2, 1.0, 0.0).astype(BF)
    c = iota((1, 64), 1)
    p = jnp.where(iota((64, 64), 0) == c % 16 * 4 + c // 16, 1.0, 0.0).astype(BF)
    projq[...] = jnp.dot(proj[...], p, preferred_element_type=F32).astype(BF)
    for layer in range(LAYERS):
        for a in range(3):
            line = [taps[layer, a * 3 + b].astype(F32) for b in range(3)]
            wall[layer, a * CHANNELS:(a + 1) * CHANNELS, :] = jnp.concatenate(line, axis=1).astype(BF)


def products(k, c, entry, rows, wbuf, share, grid, hot2):
    first = (2 * c + k) * GROUP

    def product(t, carry):
        if k == 0:
            q = t // CJ * NE + CJ * c + lax.rem(t, CJ)
        else:
            q = t // CI * NN + CI * c + lax.rem(t, CI)
        at = pl.multiple_of((first + t) * FEATS, FEATS)
        share[pl.ds(at, FEATS), :] = jnp.dot(
            rows[k, q], wbuf[entry[0, first + t]], preferred_element_type=F32)
        return carry

    lax.fori_loop(0, GROUP, product, 0, unroll=GROUP)
    half, last = divmod(c, CHUNKS // 2)
    if k == 1 or last < CHUNKS // 2 - 1:
        return
    for f in range(0, FEATS, 2):
        parts = []
        for g in (f, f + 1):
            v = share[pl.ds(half * 128 * FEATS + g, 128, stride=FEATS), :]
            hi = v.astype(BF)
            lo = (v - hi.astype(F32)).astype(BF)
            parts.append(jnp.concatenate([hi, lo], axis=0))
        r = jnp.dot(hot2[:, half * 256:half * 256 + 256], jnp.concatenate(parts, axis=1), preferred_element_type=F32)
        for g, v in ((f, r[:, :128]), (f + 1, r[:, 128:])):
            at = pl.ds(g, 128, stride=FEATS)
            grid[at, :] = v if half == 0 else grid[at, :] + v


def blend(grid, t1, t2, projq, put, send):
    tiles = []
    for wh in range(4):
        line = []
        for wl in range(4):
            wc = wh * 4 + wl
            blocks = [grid[pl.ds((wr * 16 + wc) * FEATS, FEATS), :] for wr in range(8)]
            line.append(jnp.concatenate(blocks, axis=0).astype(BF))
        tiles.append(jnp.concatenate(line, axis=1))
    y = jnp.dot(jnp.concatenate(tiles, axis=0), t1[...], preferred_element_type=F32).astype(BF)
    tiles = [
        jnp.concatenate([y[wh * 128:(wh + 1) * 128, i * 128:(i + 1) * 128] for wh in range(4)], axis=1)
        for i in range(4)
    ]
    z = jnp.dot(jnp.concatenate(tiles, axis=0), t2[...], preferred_element_type=F32).astype(BF)
    for wr in range(8):
        cells = []
        for i in range(4):
            r0 = (i * 8 + wr) * FEATS
            cells.append(jnp.concatenate(
                [z[r0:r0 + FEATS, q * 128:(q + 1) * 128] for q in range(4)], axis=0))
        o = jnp.dot(projq[...], jnp.concatenate(cells, axis=1), preferred_element_type=F32)
        o = jax.nn.gelu(o).astype(BF)
        for i in range(4):
            put(wr * 4 + i, o[:, i * 128:(i + 1) * 128])
        if wr % 2:
            send(wr // 2)


def send_halo(g, xs, strips, halo, ssem, rsem):
    n, e, up, down, left, right = places()
    lane = iota((CHANNELS, HC), 1)

    def remote(src, dst, dev, k=0):
        pltpu.make_async_remote_copy(
            src_ref=src, dst_ref=dst, send_sem=ssem.at[k], recv_sem=rsem.at[k],
            device_id=dev, device_id_type=MESH).start()

    sl = sr = jnp.zeros((CHANNELS, HC), BF)
    for k in range(8):
        v = xs[0, REACH + 8 * g + k]
        here = lane // 16 == k
        sl = jnp.where(here, pltpu.roll(v, 16 * k, 1) if k else v, sl)
        sr = jnp.where(here, pltpu.roll(v, (16 * k + 16) % HC, 1) if k < 7 else v, sr)
    strips[0, g] = sl
    strips[1, g] = sr
    for side, te in ((0, right), (1, left)):
        own = strips.at[1 - side, g]
        remote(own, halo.at[side, g + 2], (n, te))
        if g >= 2:
            remote(own, halo.at[side, g - 2], (down, te))
        else:
            remote(own, halo.at[side, g + 6], (up, te))
    if g == 1:
        remote(xs.at[0, pl.ds(REACH, REACH)], xs.at[0, pl.ds(REACH + HR, REACH)], (up, e), 1)
    if g == 3:
        remote(xs.at[0, pl.ds(HR, REACH)], xs.at[0, pl.ds(0, REACH)], (down, e), 1)


def conv(rates, wall, out, xs, es, halo, ybuf, ye, ssem, rsem):
    n, e, up, down, left, right = places()
    lane = iota((CHANNELS, HC), 1)
    row_lane = iota((1, HC), 1)

    up_ok, down_ok = jnp.where(n > 0, 1.0, 0.0), jnp.where(n < NN - 1, 1.0, 0.0)
    left_ok, right_ok = jnp.where(e > 0, 1.0, 0.0), jnp.where(e < NE - 1, 1.0, 0.0)
    part = row_lane % 64
    cols = jnp.where(part < 16, left_ok, jnp.where(part >= 48, right_ok, 1.0))

    def edge_mask(t):
        first = jnp.where(t < REACH, up_ok, 1.0)
        second = jnp.where(t + OFF >= REACH + HR, down_ok, 1.0)
        return cols * jnp.where(row_lane < 64, first, second)

    def assemble(t):
        h0, o0 = (t + 4) // 8, lax.rem(t + 4, 8)
        h1, o1 = (t + OFF + 4) // 8, lax.rem(t + OFF + 4, 8)
        a, b = xs[0, t], xs[0, t + OFF]
        pieces = [
            pltpu.roll(halo[0, h0], lax.rem(HC - 16 * o0, HC), 1), pltpu.roll(a, 16, 1),
            pltpu.roll(a, 48, 1), pltpu.roll(halo[1, h0], lax.rem(HC + 48 - 16 * o0, HC), 1),
            pltpu.roll(halo[0, h1], lax.rem(HC + 64 - 16 * o1, HC), 1), pltpu.roll(b, 80, 1),
            pltpu.roll(b, 112, 1), pltpu.roll(halo[1, h1], lax.rem(HC + 112 - 16 * o1, HC), 1),
        ]
        v = pieces[0]
        for k in range(1, 8):
            v = jnp.where(lane // 16 == k, pieces[k], v)
        es[0, t] = (v.astype(F32) * edge_mask(t)).astype(BF)

    def loop(lo, hi, body, unroll):
        lax.fori_loop(lo, hi, lambda m, carry: (body(m), carry)[1], 0, unroll=unroll)

    def total(buf, m, d):
        return buf[m - d, 0:64, :] + buf[m, 64:128, :] + buf[m + d, 128:192, :]

    def layer_ops(layer):
        d = rates[layer]
        w = wall[layer]
        y_of = ybuf.at[layer % 2]

        def one_row(m, second):
            x = xs[layer, m]
            if second is None:
                lt = rt = jnp.zeros((CHANNELS, HC), BF)
            else:
                edge = es[layer, m - OFF if second else m]
                lt = pltpu.roll(edge, d + (48 if second else 112), 1)
                rt = pltpu.roll(edge, (16 if second else 80) - d, 1)
            xl = jnp.where(lane >= d, pltpu.roll(x, d, 1), lt)
            xr = jnp.where(lane < HC - d, pltpu.roll(x, HC - d, 1), rt)
            return jnp.concatenate([xl, x, xr], axis=0)

        def one_edge(t):
            x = es[layer, t]
            return jnp.concatenate([pltpu.roll(x, d, 1), x, pltpu.roll(x, HC - d, 1)], axis=0)

        def pair(one, buf, m):
            y = jnp.dot(w, jnp.concatenate([one(m), one(m + 1)], axis=1), preferred_element_type=F32)
            buf[m] = y[:, :HC]
            buf[m + 1] = y[:, HC:]

        def rows(first, last, second):
            count = (last - first) // 2
            loop(0, count, lambda i: pair(lambda m: one_row(m, second), y_of, first + 2 * i), count)

        def edges(first, last):
            count = (last - first) // 2
            loop(0, count, lambda i: pair(one_edge, ye, first + 2 * i), count)

        def finish(m):
            v = xs[layer, m].astype(F32) + jax.nn.gelu(total(y_of, m, d))
            if layer < LAYERS - 1:
                v = v * jnp.where(m < REACH, up_ok, jnp.where(m >= REACH + HR, down_ok, 1.0))
                xs[layer + 1, m] = v.astype(BF)
            else:
                out[m - REACH] = v.astype(BF)

        def finish_edge(t):
            v = (es[layer, t].astype(F32) + jax.nn.gelu(total(ye, t, d))) * edge_mask(t)
            es[layer + 1, t] = v.astype(BF)

        def repair(second):
            def row(m):
                edge = es[layer + 1, m - OFF if second else m]
                v = xs[layer + 1, m]
                v = jnp.where(lane < 2 * HALO, pltpu.roll(edge, 48 if second else 112, 1), v)
                v = jnp.where(lane >= HC - 2 * HALO, pltpu.roll(edge, 16 if second else 80, 1), v)
                xs[layer + 1, m] = v
            return row

        return rows, edges, finish, finish_edge, repair

    arrived = [xs.at[0, pl.ds(0, 16)], xs.at[0, pl.ds(0, 2 * REACH)]]
    top, bottom = REACH, REACH + HR
    rows0, edges0, finish0, finish_edge0, _ = layer_ops(0)
    rows1, edges1, finish1, finish_edge1, repair = layer_ops(1)
    rows0(top, bottom, None)
    loop(top + HALO, bottom - HALO, finish0, 24)
    rows1(top + HALO, bottom - HALO, None)
    loop(top + 2 * HALO, bottom - 2 * HALO, finish1, 16)
    pltpu.make_async_copy(arrived[1], arrived[1], rsem.at[1]).wait()

    @pl.when(n == 0)
    def _():
        xs[0, pl.ds(0, REACH)] = jnp.zeros((REACH, CHANNELS, HC), BF)

    @pl.when(n == NN - 1)
    def _():
        xs[0, pl.ds(REACH + HR, REACH)] = jnp.zeros((REACH, CHANNELS, HC), BF)

    rows0(0, top, None)
    rows0(bottom, ROWS, None)
    loop(HALO, top + HALO, finish0, 12)
    loop(bottom - HALO, ROWS - HALO, finish0, 12)
    rows1(HALO, top + HALO, None)
    rows1(bottom - HALO, ROWS - HALO, None)
    loop(2 * HALO, top + 2 * HALO, finish1, 12)
    loop(bottom - 2 * HALO, ROWS - 2 * HALO, finish1, 12)
    pltpu.make_async_copy(arrived[0], arrived[0], rsem.at[0]).wait()
    loop(0, TILES, assemble, 12)
    edges0(0, TILES)
    loop(HALO, TILES - HALO, finish_edge0, 14)
    edges1(HALO, TILES - HALO)
    loop(2 * HALO, TILES - 2 * HALO, finish_edge1, 10)
    loop(2 * HALO, SPLIT, repair(False), 20)
    loop(SPLIT, ROWS - 2 * HALO, repair(True), 20)
    rows2, _, finish2, _, _ = layer_ops(2)
    rows2(2 * HALO, SPLIT, False)
    rows2(SPLIT, ROWS - 2 * HALO, True)
    loop(REACH, REACH + HR, finish2, 16)

    for k in range(2):
        pltpu.make_async_copy(arrived[k], arrived[k], ssem.at[k]).wait()


def kernel(pick_h, feed_h, rates_h, win_h, gates_h, w_h, proj_h, taps_h, out,
           s0, s1, m0, m1, rows, gates, wbuf, share, grid, hot2, t1, t2, projq, wall,
           xs, es, strips, halo, ybuf, ye, pick, entry, entry_v, rates, feed_v, win_v, proj, taps,
           asem, arem, ssem, rsem, lsem):
    n, e, up, down, left, right = places()
    pairs = [(pick_h, pick), (gates_h, gates), (rates_h, rates), (feed_h, feed_v), (win_h, win_v), (proj_h, proj), (taps_h, taps), (w_h, wbuf)]
    loads = [pltpu.make_async_copy(src, dst, lsem.at[k]) for k, (src, dst) in enumerate(pairs)]
    loads[0].start()
    loads[1].start()
    bar = pltpu.get_barrier_semaphore()
    for i in range(1, NE):
        pl.semaphore_signal(bar, inc=1, device_id=(n, lax.rem(e + i, NE)), device_id_type=MESH)
    for i in range(1, NN):
        pl.semaphore_signal(bar, inc=1, device_id=(lax.rem(n + i, NN), e), device_id_type=MESH)
    for tn in (up, down):
        for te in (left, right):
            pl.semaphore_signal(bar, inc=1, device_id=(tn, te), device_id_type=MESH)
    for load in loads[2:7]:
        load.start()
    loads[0].wait()
    loads[1].wait()

    def meanwhile():
        for load in loads[2:7]:
            load.wait()
        tables(win_v, feed_v, proj, taps, hot2, t1, t2, projq, wall, entry_v)
        to_scalar = pltpu.make_async_copy(entry_v, entry, lsem.at[8])
        to_scalar.start()
        to_scalar.wait()
        loads[7].wait()

    sent = exchange(pick, gates, s0, s1, m0, m1, rows, asem, arem, bar, loads[7].start, meanwhile,
                    lambda k, c: products(k, c, entry, rows, wbuf, share, grid, hot2))

    def put(i, v):
        xs[0, i + REACH] = v

    blend(grid, t1, t2, projq, put,
          lambda g: send_halo(g, xs, strips, halo, ssem, rsem))
    conv(rates, wall, out, xs, es, halo, ybuf, ye, ssem, rsem)
    sent()


def per_device(gates, mixing_weight_blocks, send_pick, feed, window, proj_weight, conv_weight, rates):
    hbm = pl.BlockSpec(memory_space=pltpu.HBM)
    blk = (FEATS, GATES)
    return pl.pallas_call(
        kernel,
        out_shape=jax.ShapeDtypeStruct((HR, CHANNELS, HC), BF),
        in_specs=[hbm] * 8,
        out_specs=pl.BlockSpec(memory_space=pltpu.VMEM),
        scratch_shapes=[
            pltpu.VMEM((NE, NN) + blk, BF), pltpu.VMEM((NN, NE) + blk, BF),
            pltpu.VMEM((NE, NN) + blk, BF), pltpu.VMEM((NN, NE) + blk, BF),
            pltpu.VMEM((2, ND) + blk, BF), pltpu.VMEM((PMAX,) + blk, BF),
            pltpu.VMEM((PMAX, GATES, 128), BF),
            pltpu.VMEM((PMAX * FEATS, 128), F32),
            pltpu.VMEM((128 * FEATS, 128), F32),
            pltpu.VMEM((128, 512), BF), pltpu.VMEM((512, 512), BF), pltpu.VMEM((512, 512), BF),
            pltpu.VMEM((CHANNELS, 64), BF), pltpu.VMEM((LAYERS, 3 * CHANNELS, 3 * CHANNELS), BF),
            pltpu.VMEM((LAYERS, ROWS, CHANNELS, HC), BF),
            pltpu.VMEM((LAYERS, TILES, CHANNELS, HC), BF),
            pltpu.VMEM((2, HR // 8, CHANNELS, HC), BF),
            pltpu.VMEM((2, 8, CHANNELS, HC), BF),
            pltpu.VMEM((2, ROWS, 3 * CHANNELS, HC), F32),
            pltpu.VMEM((TILES, 3 * CHANNELS, HC), F32),
            pltpu.SMEM((1, 2, ND), jnp.int32), pltpu.SMEM((1, PMAX), jnp.int32), pltpu.VMEM((1, PMAX), jnp.int32),
            pltpu.SMEM((LAYERS,), jnp.int32), pltpu.VMEM((1, PMAX), jnp.int32), pltpu.VMEM((1, PMAX), jnp.int32),
            pltpu.VMEM((CHANNELS, 64), BF), pltpu.VMEM((LAYERS, 9, CHANNELS, CHANNELS), BF),
            pltpu.SemaphoreType.DMA((4 * CHUNKS,)), pltpu.SemaphoreType.DMA((4 * CHUNKS,)),
            pltpu.SemaphoreType.DMA((2,)), pltpu.SemaphoreType.DMA((2,)),
            pltpu.SemaphoreType.DMA((9,)),
        ],
        compiler_params=pltpu.CompilerParams(
            collective_id=0, has_side_effects=True, vmem_limit_bytes=58 << 20),
        name="radar",
    )(send_pick.transpose(0, 2, 1), feed, rates, window, gates, mixing_weight_blocks, proj_weight, conv_weight).transpose(1, 0, 2)


def solution(mesh):
    in_specs = (
        P(("north", "east"), None, None),
        P(("north", "east"), None, None),
        P(("north", "east"), None, None),
        P(("north", "east"), None),
        P(("north", "east"), None),
        P(),
        P(),
        P(),
    )
    return jax.shard_map(
        per_device, mesh=mesh, in_specs=in_specs, out_specs=P(None, "north", "east"), check_vma=False
    )
```

```python
import functools

import jax
import jax.numpy as jnp
from jax import lax
from jax.experimental import pallas as pl
from jax.experimental.pallas import tpu as pltpu
from jax.sharding import PartitionSpec as P

MESH = pl.DeviceIdType.MESH
NN, NE = 8, 16
ND = NN * NE
GATES = 128
FEATS = 16
CHANNELS = 64
LAYERS = 3
HALO = 4
HR, HC = 32, 128
PMAX = 256
BF, F32 = jnp.bfloat16, jnp.float32


CHUNKS = 4
CI, CJ = NN // CHUNKS, NE // CHUNKS
GROUP = CI * NE
REACH = LAYERS * HALO
ROWS = HR + 2 * REACH
TILES, OFF, SPLIT = 36, 20, 28


def iota(shape, dim):
    return lax.broadcasted_iota(jnp.int32, shape, dim)


def places():
    n, e = lax.axis_index("north"), lax.axis_index("east")
    up, down = lax.rem(n + NN - 1, NN), lax.rem(n + 1, NN)
    left, right = lax.rem(e + NE - 1, NE), lax.rem(e + 1, NE)
    return n, e, up, down, left, right


def exchange(pick, gates, s0, s1, m0, m1, rows, ssem, rsem, bar, gathered, meanwhile, arrived):
    n, e, up, down, left, right = places()
    f0, f1 = rows.at[0], rows.at[1]

    def gather(t, carry):
        i, j = t // NE, lax.rem(t, NE)
        at = lax.rem(n + i, NN) * NE + lax.rem(e + j, NE)
        for k in range(2):
            p = pick[0, k, at]
            v = gates[jnp.maximum(p, 0)]
            v = jnp.where(p >= 0, v, jnp.zeros_like(v))
            if k == 0:
                s0[j, i] = v
            else:
                s1[i, j] = v
        return carry

    lax.fori_loop(0, ND, gather, 0, unroll=64)
    gathered()
    pl.semaphore_wait(bar, NE + NN - 2 + 4)

    def remote(src, dst, k, i, j):
        pltpu.make_async_remote_copy(
            src_ref=src, dst_ref=dst, send_sem=ssem.at[k], recv_sem=rsem.at[k],
            device_id=(lax.rem(n + i, NN), lax.rem(e + j, NE)), device_id_type=MESH,
        ).start()

    for c in range(CHUNKS):
        for j in range(max(1, CJ * c), CJ * c + CJ):
            remote(s0.at[j], m0.at[j], c, 0, j)
            i = j // 2
            if j % 2 == 0 and i > 0:
                remote(s1.at[i], m1.at[i], CHUNKS + c, i, 0)
    m0[0] = s0[0]
    m1[0] = s1[0]
    meanwhile()

    def wait(count, sem):
        r = rows.at[0, pl.ds(0, count)]
        pltpu.make_async_copy(r, r, sem).wait()

    a_counts = [(CJ - (c == 0)) * NN for c in range(CHUNKS)] + [(CI - (c == 0)) * NE for c in range(CHUNKS)]
    b_counts = [(NN - 1) * CJ] * CHUNKS + [(NE - 1) * CI] * CHUNKS
    counts = a_counts + b_counts
    for c in range(CHUNKS):
        wait(counts[CHUNKS + c], rsem.at[CHUNKS + c])
        for j in range(1, NE):
            remote(m1.at[pl.ds(CI * c, CI), j], f1.at[pl.ds(j * NN + CI * c, CI)], 3 * CHUNKS + c, 0, j)
        f1[pl.ds(CI * c, CI)] = m1[pl.ds(CI * c, CI), 0]
        wait(counts[c], rsem.at[c])
        for i in range(1, NN):
            remote(m0.at[pl.ds(CJ * c, CJ), i], f0.at[pl.ds(i * NE + CJ * c, CJ)], 2 * CHUNKS + c, i, 0)
        f0[pl.ds(CJ * c, CJ)] = m0[pl.ds(CJ * c, CJ), 0]
    for c in range(CHUNKS):
        for k in (1, 0):
            at = (2 + k) * CHUNKS + c
            wait(counts[at], rsem.at[at])
            arrived(k, c)

    def sent():
        for k, count in enumerate(counts):
            wait(count, ssem.at[k])

    return sent


def tables(win_v, feed_v, proj, taps, hot2, t1, t2, projq, wall, entry):
    n, e, *_ = places()
    feed = feed_v[...]
    s, k = feed // 2, feed % 2
    i, j = (n + NN - s // NE) % NN, (e + NE - s % NE) % NE
    q0 = j // CJ * 2 * GROUP + i * CJ + j % CJ
    q1 = i // CI * 2 * GROUP + GROUP + j * CI + i % CI
    q = jnp.where(feed < 0, -1, jnp.where(k == 0, q0, q1))
    down_q = jnp.transpose(jnp.broadcast_to(q, (128, PMAX)))
    number = iota((PMAX, 128), 0)
    uses = []
    for h in range(2):
        same = down_q == iota((PMAX, 128), 1) + 128 * h
        entry[:, h * 128:(h + 1) * 128] = jnp.max(jnp.where(same, number, 0), axis=0, keepdims=True)
        uses.append(jnp.where(same, 1.0, 0.0).astype(BF))
    hot = jnp.where(win_v[...] == iota((GATES, PMAX), 0), 1.0, 0.0).astype(BF)
    hot = jnp.dot(hot, jnp.concatenate(uses, axis=1), preferred_element_type=F32).astype(BF)
    hot2[...] = jnp.concatenate([hot[:, :128], hot[:, :128], hot[:, 128:], hot[:, 128:]], axis=1)
    col = iota((1, 512), 1)
    i1, w1, a1, b1, j1 = col // 128, col // 32 % 4, col // 16 % 2, col // 8 % 2, col % 8
    src1 = w1 * 128 + i1 * 32 + a1 * 16 + j1 * 2 + b1
    t1[...] = jnp.where(iota((512, 512), 0) == src1, 1.0, 0.0).astype(BF)
    q2, wh2, wl2, j2 = col // 128, col // 32 % 4, col // 8 % 4, col % 8
    src2 = wh2 * 128 + wl2 * 32 + q2 * 8 + j2
    t2[...] = jnp.where(iota((512, 512), 0) == src2, 1.0, 0.0).astype(BF)
    c = iota((1, 64), 1)
    p = jnp.where(iota((64, 64), 0) == c % 16 * 4 + c // 16, 1.0, 0.0).astype(BF)
    projq[...] = jnp.dot(proj[...], p, preferred_element_type=F32).astype(BF)
    for layer in range(LAYERS):
        for a in range(3):
            line = [taps[layer, a * 3 + b].astype(F32) for b in range(3)]
            wall[layer, a * CHANNELS:(a + 1) * CHANNELS, :] = jnp.concatenate(line, axis=1).astype(BF)


def products(k, c, entry, rows, wbuf, share, grid, hot2):
    first = (2 * c + k) * GROUP

    def product(t, carry):
        if k == 0:
            q = t // CJ * NE + CJ * c + lax.rem(t, CJ)
        else:
            q = t // CI * NN + CI * c + lax.rem(t, CI)
        at = pl.multiple_of((first + t) * FEATS, FEATS)
        share[pl.ds(at, FEATS), :] = jnp.dot(
            rows[k, q], wbuf[entry[0, first + t]], preferred_element_type=F32)
        return carry

    lax.fori_loop(0, GROUP, product, 0, unroll=GROUP)
    half, last = divmod(c, CHUNKS // 2)
    if k == 1 or last < CHUNKS // 2 - 1:
        return
    for f in range(0, FEATS, 2):
        parts = []
        for g in (f, f + 1):
            v = share[pl.ds(half * 128 * FEATS + g, 128, stride=FEATS), :]
            hi = v.astype(BF)
            lo = (v - hi.astype(F32)).astype(BF)
            parts.append(jnp.concatenate([hi, lo], axis=0))
        r = jnp.dot(hot2[:, half * 256:half * 256 + 256], jnp.concatenate(parts, axis=1), preferred_element_type=F32)
        for g, v in ((f, r[:, :128]), (f + 1, r[:, 128:])):
            at = pl.ds(g, 128, stride=FEATS)
            grid[at, :] = v if half == 0 else grid[at, :] + v


def blend(grid, t1, t2, projq, put, send):
    tiles = []
    for wh in range(4):
        line = []
        for wl in range(4):
            wc = wh * 4 + wl
            blocks = [grid[pl.ds((wr * 16 + wc) * FEATS, FEATS), :] for wr in range(8)]
            line.append(jnp.concatenate(blocks, axis=0).astype(BF))
        tiles.append(jnp.concatenate(line, axis=1))
    y = jnp.dot(jnp.concatenate(tiles, axis=0), t1[...], preferred_element_type=F32).astype(BF)
    tiles = [
        jnp.concatenate([y[wh * 128:(wh + 1) * 128, i * 128:(i + 1) * 128] for wh in range(4)], axis=1)
        for i in range(4)
    ]
    z = jnp.dot(jnp.concatenate(tiles, axis=0), t2[...], preferred_element_type=F32).astype(BF)
    for wr in range(8):
        cells = []
        for i in range(4):
            r0 = (i * 8 + wr) * FEATS
            cells.append(jnp.concatenate(
                [z[r0:r0 + FEATS, q * 128:(q + 1) * 128] for q in range(4)], axis=0))
        o = jnp.dot(projq[...], jnp.concatenate(cells, axis=1), preferred_element_type=F32)
        o = jax.nn.gelu(o).astype(BF)
        for i in range(4):
            put(wr * 4 + i, o[:, i * 128:(i + 1) * 128])
        if wr % 2:
            send(wr // 2)


def send_halo(g, xs, strips, halo, ssem, rsem):
    n, e, up, down, left, right = places()
    lane = iota((CHANNELS, HC), 1)

    def remote(src, dst, dev, k=0):
        pltpu.make_async_remote_copy(
            src_ref=src, dst_ref=dst, send_sem=ssem.at[k], recv_sem=rsem.at[k],
            device_id=dev, device_id_type=MESH).start()

    if g == 1:
        remote(xs.at[0, pl.ds(REACH, REACH)], xs.at[0, pl.ds(REACH + HR, REACH)], (up, e), 1)
    if g == 3:
        remote(xs.at[0, pl.ds(HR, REACH)], xs.at[0, pl.ds(0, REACH)], (down, e), 1)
    sl = sr = jnp.zeros((CHANNELS, HC), BF)
    for k in range(8):
        v = xs[0, REACH + 8 * g + k]
        here = lane // 16 == k
        sl = jnp.where(here, pltpu.roll(v, 16 * k, 1) if k else v, sl)
        sr = jnp.where(here, pltpu.roll(v, (16 * k + 16) % HC, 1) if k < 7 else v, sr)
    strips[0, g] = sl
    strips[1, g] = sr
    for side, te in ((0, right), (1, left)):
        own = strips.at[1 - side, g]
        remote(own, halo.at[side, g + 2], (n, te))
        if g >= 2:
            remote(own, halo.at[side, g - 2], (down, te))
        else:
            remote(own, halo.at[side, g + 6], (up, te))


def conv(rates, wall, out, xs, es, halo, ybuf, ye, ssem, rsem):
    n, e, up, down, left, right = places()
    lane = iota((CHANNELS, HC), 1)
    row_lane = iota((1, HC), 1)

    up_ok, down_ok = jnp.where(n > 0, 1.0, 0.0), jnp.where(n < NN - 1, 1.0, 0.0)
    left_ok, right_ok = jnp.where(e > 0, 1.0, 0.0), jnp.where(e < NE - 1, 1.0, 0.0)
    part = row_lane % 64
    cols = jnp.where(part < 16, left_ok, jnp.where(part >= 48, right_ok, 1.0))

    def edge_mask(t):
        first = jnp.where(t < REACH, up_ok, 1.0)
        second = jnp.where(t + OFF >= REACH + HR, down_ok, 1.0)
        return cols * jnp.where(row_lane < 64, first, second)

    def assemble(t):
        h0, o0 = (t + 4) // 8, lax.rem(t + 4, 8)
        h1, o1 = (t + OFF + 4) // 8, lax.rem(t + OFF + 4, 8)
        a, b = xs[0, t], xs[0, t + OFF]
        pieces = [
            pltpu.roll(halo[0, h0], lax.rem(HC - 16 * o0, HC), 1), pltpu.roll(a, 16, 1),
            pltpu.roll(a, 48, 1), pltpu.roll(halo[1, h0], lax.rem(HC + 48 - 16 * o0, HC), 1),
            pltpu.roll(halo[0, h1], lax.rem(HC + 64 - 16 * o1, HC), 1), pltpu.roll(b, 80, 1),
            pltpu.roll(b, 112, 1), pltpu.roll(halo[1, h1], lax.rem(HC + 112 - 16 * o1, HC), 1),
        ]
        v = pieces[0]
        for k in range(1, 8):
            v = jnp.where(lane // 16 == k, pieces[k], v)
        es[0, t] = (v.astype(F32) * edge_mask(t)).astype(BF)

    def loop(lo, hi, body, unroll):
        lax.fori_loop(lo, hi, lambda m, carry: (body(m), carry)[1], 0, unroll=unroll)

    def total(buf, m, d):
        return buf[m - d, 0:64, :] + buf[m, 64:128, :] + buf[m + d, 128:192, :]

    def layer_ops(layer):
        d = rates[layer]
        w = wall[layer]
        y_of = ybuf.at[layer % 2]

        def one_row(m, second):
            x = xs[layer, m]
            if second is None:
                lt = rt = jnp.zeros((CHANNELS, HC), BF)
            else:
                edge = es[layer, m - OFF if second else m]
                lt = pltpu.roll(edge, d + (48 if second else 112), 1)
                rt = pltpu.roll(edge, (16 if second else 80) - d, 1)
            xl = jnp.where(lane >= d, pltpu.roll(x, d, 1), lt)
            xr = jnp.where(lane < HC - d, pltpu.roll(x, HC - d, 1), rt)
            return jnp.concatenate([xl, x, xr], axis=0)

        def one_edge(t):
            x = es[layer, t]
            return jnp.concatenate([pltpu.roll(x, d, 1), x, pltpu.roll(x, HC - d, 1)], axis=0)

        def pair(one, buf, m):
            y = jnp.dot(w, jnp.concatenate([one(m), one(m + 1)], axis=1), preferred_element_type=F32)
            buf[m] = y[:, :HC]
            buf[m + 1] = y[:, HC:]

        def rows(first, last, second):
            count = (last - first) // 2
            loop(0, count, lambda i: pair(lambda m: one_row(m, second), y_of, first + 2 * i), count)

        def edges(first, last):
            count = (last - first) // 2
            loop(0, count, lambda i: pair(one_edge, ye, first + 2 * i), count)

        def finish(m):
            v = xs[layer, m].astype(F32) + jax.nn.gelu(total(y_of, m, d))
            if layer < LAYERS - 1:
                v = v * jnp.where(m < REACH, up_ok, jnp.where(m >= REACH + HR, down_ok, 1.0))
                xs[layer + 1, m] = v.astype(BF)
            else:
                out[m - REACH] = v.astype(BF)

        def finish_edge(t):
            v = (es[layer, t].astype(F32) + jax.nn.gelu(total(ye, t, d))) * edge_mask(t)
            es[layer + 1, t] = v.astype(BF)

        def repair(second):
            def row(m):
                edge = es[layer + 1, m - OFF if second else m]
                v = xs[layer + 1, m]
                v = jnp.where(lane < 2 * HALO, pltpu.roll(edge, 48 if second else 112, 1), v)
                v = jnp.where(lane >= HC - 2 * HALO, pltpu.roll(edge, 16 if second else 80, 1), v)
                xs[layer + 1, m] = v
            return row

        return rows, edges, finish, finish_edge, repair

    arrived = [xs.at[0, pl.ds(0, 16)], xs.at[0, pl.ds(0, 2 * REACH)]]
    top, bottom = REACH, REACH + HR
    rows0, edges0, finish0, finish_edge0, _ = layer_ops(0)
    rows1, edges1, finish1, finish_edge1, repair = layer_ops(1)
    rows0(top, bottom, None)
    loop(top + HALO, bottom - HALO, finish0, 24)
    rows1(top + HALO, bottom - HALO, None)
    loop(top + 2 * HALO, bottom - 2 * HALO, finish1, 16)
    pltpu.make_async_copy(arrived[1], arrived[1], rsem.at[1]).wait()

    @pl.when(n == 0)
    def _():
        xs[0, pl.ds(0, REACH)] = jnp.zeros((REACH, CHANNELS, HC), BF)

    @pl.when(n == NN - 1)
    def _():
        xs[0, pl.ds(REACH + HR, REACH)] = jnp.zeros((REACH, CHANNELS, HC), BF)

    rows0(0, top, None)
    rows0(bottom, ROWS, None)
    loop(HALO, top + HALO, finish0, 12)
    loop(bottom - HALO, ROWS - HALO, finish0, 12)
    rows1(HALO, top + HALO, None)
    rows1(bottom - HALO, ROWS - HALO, None)
    loop(2 * HALO, top + 2 * HALO, finish1, 12)
    loop(bottom - 2 * HALO, ROWS - 2 * HALO, finish1, 12)
    pltpu.make_async_copy(arrived[0], arrived[0], rsem.at[0]).wait()
    loop(0, TILES, assemble, 36)
    edges0(0, TILES)
    loop(HALO, TILES - HALO, finish_edge0, 28)
    edges1(HALO, TILES - HALO)
    loop(2 * HALO, TILES - 2 * HALO, finish_edge1, 20)
    loop(2 * HALO, SPLIT, repair(False), 20)
    loop(SPLIT, ROWS - 2 * HALO, repair(True), 20)
    rows2, _, finish2, _, _ = layer_ops(2)
    rows2(2 * HALO, SPLIT, False)
    rows2(SPLIT, ROWS - 2 * HALO, True)
    loop(REACH, REACH + HR, finish2, 32)

    for k in range(2):
        pltpu.make_async_copy(arrived[k], arrived[k], ssem.at[k]).wait()


def kernel(pick_h, feed_h, rates_h, win_h, gates_h, w_h, proj_h, taps_h, out,
           s0, s1, m0, m1, rows, gates, wbuf, share, grid, hot2, t1, t2, projq, wall,
           xs, es, strips, halo, ybuf, ye, pick, entry, entry_v, rates, feed_v, win_v, proj, taps,
           asem, arem, ssem, rsem, lsem):
    n, e, up, down, left, right = places()
    pairs = [(pick_h, pick), (gates_h, gates), (rates_h, rates), (feed_h, feed_v), (win_h, win_v), (proj_h, proj), (taps_h, taps), (w_h, wbuf)]
    loads = [pltpu.make_async_copy(src, dst, lsem.at[k]) for k, (src, dst) in enumerate(pairs)]
    loads[0].start()
    loads[1].start()
    bar = pltpu.get_barrier_semaphore()
    for i in range(1, NE):
        pl.semaphore_signal(bar, inc=1, device_id=(n, lax.rem(e + i, NE)), device_id_type=MESH)
    for i in range(1, NN):
        pl.semaphore_signal(bar, inc=1, device_id=(lax.rem(n + i, NN), e), device_id_type=MESH)
    for tn in (up, down):
        for te in (left, right):
            pl.semaphore_signal(bar, inc=1, device_id=(tn, te), device_id_type=MESH)
    for load in loads[2:7]:
        load.start()
    loads[0].wait()
    loads[1].wait()

    def meanwhile():
        for load in loads[2:7]:
            load.wait()
        tables(win_v, feed_v, proj, taps, hot2, t1, t2, projq, wall, entry_v)
        to_scalar = pltpu.make_async_copy(entry_v, entry, lsem.at[8])
        to_scalar.start()
        to_scalar.wait()
        loads[7].wait()

    sent = exchange(pick, gates, s0, s1, m0, m1, rows, asem, arem, bar, loads[7].start, meanwhile,
                    lambda k, c: products(k, c, entry, rows, wbuf, share, grid, hot2))

    def put(i, v):
        xs[0, i + REACH] = v

    blend(grid, t1, t2, projq, put,
          lambda g: send_halo(g, xs, strips, halo, ssem, rsem))
    conv(rates, wall, out, xs, es, halo, ybuf, ye, ssem, rsem)
    sent()


def per_device(gates, mixing_weight_blocks, send_pick, feed, window, proj_weight, conv_weight, rates):
    hbm = pl.BlockSpec(memory_space=pltpu.HBM)
    blk = (FEATS, GATES)
    return pl.pallas_call(
        kernel,
        out_shape=jax.ShapeDtypeStruct((HR, CHANNELS, HC), BF),
        in_specs=[hbm] * 8,
        out_specs=pl.BlockSpec(memory_space=pltpu.VMEM),
        scratch_shapes=[
            pltpu.VMEM((NE, NN) + blk, BF), pltpu.VMEM((NN, NE) + blk, BF),
            pltpu.VMEM((NE, NN) + blk, BF), pltpu.VMEM((NN, NE) + blk, BF),
            pltpu.VMEM((2, ND) + blk, BF), pltpu.VMEM((PMAX,) + blk, BF),
            pltpu.VMEM((PMAX, GATES, 128), BF),
            pltpu.VMEM((PMAX * FEATS, 128), F32),
            pltpu.VMEM((128 * FEATS, 128), F32),
            pltpu.VMEM((128, 512), BF), pltpu.VMEM((512, 512), BF), pltpu.VMEM((512, 512), BF),
            pltpu.VMEM((CHANNELS, 64), BF), pltpu.VMEM((LAYERS, 3 * CHANNELS, 3 * CHANNELS), BF),
            pltpu.VMEM((LAYERS, ROWS, CHANNELS, HC), BF),
            pltpu.VMEM((LAYERS, TILES, CHANNELS, HC), BF),
            pltpu.VMEM((2, HR // 8, CHANNELS, HC), BF),
            pltpu.VMEM((2, 8, CHANNELS, HC), BF),
            pltpu.VMEM((2, ROWS, 3 * CHANNELS, HC), F32),
            pltpu.VMEM((TILES, 3 * CHANNELS, HC), F32),
            pltpu.SMEM((1, 2, ND), jnp.int32), pltpu.SMEM((1, PMAX), jnp.int32), pltpu.VMEM((1, PMAX), jnp.int32),
            pltpu.SMEM((LAYERS,), jnp.int32), pltpu.VMEM((1, PMAX), jnp.int32), pltpu.VMEM((1, PMAX), jnp.int32),
            pltpu.VMEM((CHANNELS, 64), BF), pltpu.VMEM((LAYERS, 9, CHANNELS, CHANNELS), BF),
            pltpu.SemaphoreType.DMA((4 * CHUNKS,)), pltpu.SemaphoreType.DMA((4 * CHUNKS,)),
            pltpu.SemaphoreType.DMA((2,)), pltpu.SemaphoreType.DMA((2,)),
            pltpu.SemaphoreType.DMA((9,)),
        ],
        compiler_params=pltpu.CompilerParams(
            collective_id=0, has_side_effects=True, vmem_limit_bytes=58 << 20),
        name="radar",
    )(send_pick.transpose(0, 2, 1), feed, rates, window, gates, mixing_weight_blocks, proj_weight, conv_weight).transpose(1, 0, 2)


def solution(mesh):
    in_specs = (
        P(("north", "east"), None, None),
        P(("north", "east"), None, None),
        P(("north", "east"), None, None),
        P(("north", "east"), None),
        P(("north", "east"), None),
        P(),
        P(),
        P(),
    )
    return jax.shard_map(
        per_device, mesh=mesh, in_specs=in_specs, out_specs=P(None, "north", "east"), check_vma=False
    )
```
